256 devices in a mesh: section: 16 (over y_lo, z), tensor: 16 (over x, y_hi, core).
Axes of the slice: x: 4, y: 4 (y_hi: 2, y_lo: 2; y = y_hi * 2 + y_lo), z: 8, core: 2. Of those that a mesh axis runs over, the one named last changes fastest.
Arguments:
- initial_stack_inputs: bfloat16 [3072, 8192], P('section', 'tensor'), may hold values from -54 to 54
- initial_sequence_starts: int32 [16], P('section'), may hold values 0 or 1
- arriving_pieces: bfloat16 [384, 8192], P(None, 'tensor'), may hold values from -54 to 54
- recall_embeddings: bfloat16 [64, 8192], P(None, 'tensor'), may hold values from -54 to 54
- rescaling_factors: float32 [16, 8192], P('section'), may hold values from 0.5 to 1.5
- lookup_projection: bfloat16 [16, 8192, 4096], P('section', None, 'tensor'), may hold values from -0.25 to 0.25
- content_projection: bfloat16 [16, 8192, 4096], P('section', None, 'tensor'), may hold values from -0.25 to 0.25
- write_gate_projection: bfloat16 [16, 8192, 32], P('section', None, 'tensor'), may hold values from -0.25 to 0.25
- final_projection: bfloat16 [16, 4096, 8192], P('section', 'tensor'), may hold values from -0.125 to 0.125
- associative_stores: float32 [16, 32, 128, 128], P('section', 'tensor'), may hold values from -7680 to 7680
- denominator_vectors: float32 [16, 32, 128], P('section', 'tensor'), may hold values from 50 to 200
Outputs:
- wave_front: bfloat16 [3072, 8192], P('section', 'tensor')
The draws below stay inside these ranges and needn't reach their ends.
All inputs are finite; a program needn't handle non-finite values. No bound on the sum of `initial_sequence_starts` on one device may be relied on, other than what follows from the above.
Results may differ from the reference program's by a relative error of at most 0.022.
Values may be sent and summed in bfloat16 or wider, within the bound.
No kernel may reach another device: no remote copies, remote signals or barrier semaphores. Data moves between devices by JAX's collectives and lax.ppermute only.
A program may use at most 64 MiB of HBM per device.

```python
import math
import jax
import jax.numpy as jnp
from jax import lax

HIDDEN_DIMENSION = 8192
H = 32
HD = 128
SEG = 128
MEM = 64
STEPS = 4
HK = 4096
PIECE_LENGTH = 192
DEPTH_TOTAL = 16
N_TENSOR = 16


def spread_scales(key, noise):
    first_key, second_key = jax.random.split(key)
    log_low = math.log(0.3)
    log_high = math.log(3.0)
    row_scale = jnp.exp(jax.random.uniform(first_key, (noise.shape[0], 1), jnp.float32, log_low, log_high))
    col_scale = jnp.exp(jax.random.uniform(second_key, (1, noise.shape[1]), jnp.float32, log_low, log_high))
    return (noise * row_scale * col_scale).astype(jnp.bfloat16)


def draw_initial_stack_inputs(key, part):
    key = jax.random.fold_in(key, 11)
    noise_key, scale_key = jax.random.split(key, 2)
    array_shape = (DEPTH_TOTAL * PIECE_LENGTH, HIDDEN_DIMENSION)
    noise = jnp.clip(jax.random.normal(noise_key, array_shape, jnp.float32), -6.0, 6.0)
    return spread_scales(scale_key, noise)


def draw_arriving_pieces(key, part):
    key = jax.random.fold_in(key, 12)
    noise_key, scale_key = jax.random.split(key, 2)
    array_shape = ((STEPS - 1) * SEG, HIDDEN_DIMENSION)
    noise = jnp.clip(jax.random.normal(noise_key, array_shape, jnp.float32), -6.0, 6.0)
    return spread_scales(scale_key, noise)


def draw_recall_embeddings(key, part):
    key = jax.random.fold_in(key, 13)
    noise_key, scale_key = jax.random.split(key, 2)
    array_shape = (MEM, HIDDEN_DIMENSION)
    noise = jnp.clip(jax.random.normal(noise_key, array_shape, jnp.float32), -6.0, 6.0)
    return spread_scales(scale_key, noise)


def with_ends(array, own_key, smallest, top_value):
    longest = array.shape.index(max(array.shape))
    spots = []
    for shift in (0, 1):
        where = [jax.random.randint(jax.random.fold_in(own_key, axis), (), 0, length) for axis, length in enumerate(array.shape)]
        where[longest] = (where[longest] + shift) % array.shape[longest]
        spots.append(tuple(where))
    return array.at[spots[0]].set(smallest).at[spots[1]].set(top_value)


def spiked(entries, key, source, target, shards_of, factor):
    def block_of(position):
        return (jnp.arange(entries.shape[position]) // (entries.shape[position] // shards_of)).reshape((-1,) + (1,) * (entries.ndim - 1 - position))

    near = jax.random.permutation(key, shards_of)[block_of(target)]
    second = (block_of(target) + shards_of // 2) % shards_of
    return jnp.where((block_of(source) == near) | (block_of(source) == second), factor * entries, entries)


def shard_levels(key, shape, cuts, smallest, largest):
    loudness, own = 1.0, jax.random.fold_in(key, 6)
    for axis_at, blocks in cuts:
        draws = jnp.exp(jax.random.uniform(jax.random.fold_in(own, axis_at), (blocks,), jnp.float32, smallest / len(cuts), largest / len(cuts)))
        loudness = loudness * jnp.repeat(draws, shape[axis_at] // blocks).reshape([-1 if axis == axis_at else 1 for axis in range(len(shape))])
    return loudness


def gaussian(own_key, shape, width, bound, pieces=(), kind=jnp.bfloat16):
    entries = width * jax.random.normal(own_key, shape, jnp.float32)
    if pieces:
        entries = entries * shard_levels(own_key, shape, pieces, -0.22, 0.18)
    return jnp.clip(entries, -bound, bound).astype(kind)


def heavy_noise(key, shape, spread, most, shards, heavy, kind=jnp.bfloat16):
    values = spread * jax.random.normal(key, shape, jnp.float32)
    if shards:
        values = values * shard_levels(key, shape, shards, -0.22, 0.18)
    return jnp.clip(spiked(values, jax.random.fold_in(key, 3), *heavy), -most, most).astype(kind)


def setup_inputs(seed: int = 0) -> dict:
    arg_keys = jax.random.split(jax.random.key(seed), 12)
    initial_stack_inputs = draw_initial_stack_inputs(jax.random.fold_in(arg_keys[11], 71), 0)
    initial_sequence_starts = with_ends((jax.random.randint(arg_keys[1], (DEPTH_TOTAL,), 0, 4) < 1).astype(jnp.int32), jax.random.fold_in(arg_keys[1], 1), 0, 1)
    arriving_pieces = draw_arriving_pieces(jax.random.fold_in(arg_keys[11], 71), 0)
    recall_embeddings = draw_recall_embeddings(jax.random.fold_in(arg_keys[11], 71), 0)
    rescaling_factors = jnp.clip(1.0 + 0.1 * jax.random.normal(arg_keys[4], (DEPTH_TOTAL, HIDDEN_DIMENSION), jnp.float32), 0.5, 1.5)
    lookup_projection = gaussian(arg_keys[5], (DEPTH_TOTAL, HIDDEN_DIMENSION, HK), (HIDDEN_DIMENSION // 16) ** -0.5, 0.25, ((0, 16), (2, 16)))
    content_projection = gaussian(arg_keys[6], (DEPTH_TOTAL, HIDDEN_DIMENSION, HK), (HIDDEN_DIMENSION // 16) ** -0.5, 0.25, ((0, 16), (2, 16)))
    write_gate_projection = gaussian(arg_keys[7], (DEPTH_TOTAL, HIDDEN_DIMENSION, H), (HIDDEN_DIMENSION // 16) ** -0.5, 0.25, ((0, 16), (2, 16)))
    final_projection = heavy_noise(arg_keys[8], (DEPTH_TOTAL, HK, HIDDEN_DIMENSION), HK ** -0.5, 0.125, ((0, 16), (1, 16)), (1, 2, 16, 2.0))
    associative_stores = gaussian(arg_keys[9], (DEPTH_TOTAL, H, HD, HD), (10 * HD), 7680.0, ((0, 16), (1, 16)), jnp.float32)
    denominator_vectors = jnp.clip(jnp.exp(math.log(200.0) - 1.3862944 * jax.random.uniform(arg_keys[10], (DEPTH_TOTAL, H, HD), jnp.float32) ** shard_levels(arg_keys[10], (DEPTH_TOTAL, H, HD), ((0, 16), (1, 16)), -0.2, 0.2)), 50.0, 200.0)
    return {"initial_stack_inputs": initial_stack_inputs, "initial_sequence_starts": initial_sequence_starts, "arriving_pieces": arriving_pieces, "recall_embeddings": recall_embeddings, "rescaling_factors": rescaling_factors, "lookup_projection": lookup_projection, "content_projection": content_projection, "write_gate_projection": write_gate_projection, "final_projection": final_projection, "associative_stores": associative_stores, "denominator_vectors": denominator_vectors}


EPS = 1e-05

def feature_map(values):
    return jax.nn.elu(values) + 1.0

def section_layer(inputs, write):
    rows_in, sequence_begin_flag, rescaling_factors, lookup_projection, content_projection, write_gate_projection, final_projection, memory_matrix, denominator_vectors = inputs
    retained = (1 - sequence_begin_flag).astype(jnp.float32)
    memory_matrix = memory_matrix * retained
    denominator_vectors = denominator_vectors * retained
    widened = rows_in.astype(jnp.float32)
    row_scale = lax.rsqrt(lax.optimization_barrier(jnp.mean(widened * widened, axis=1, keepdims=True)) + EPS)
    normed = (widened * row_scale * rescaling_factors).astype(jnp.bfloat16)
    mapped_keys = feature_map(jnp.dot(normed, lookup_projection, preferred_element_type=jnp.float32)).reshape(PIECE_LENGTH, H, HD)
    values = jnp.dot(normed, content_projection, preferred_element_type=jnp.float32).reshape(PIECE_LENGTH, H, HD)
    readout_numerator = jnp.einsum('dyt,ytn->dyn', mapped_keys, memory_matrix, precision=lax.Precision.HIGHEST)
    denominator = jnp.einsum('rhk,hk->rh', mapped_keys, denominator_vectors, precision=lax.Precision.HIGHEST) + 1.0
    readout = readout_numerator / denominator[:, :, None]
    rounded = readout.astype(jnp.bfloat16).reshape(PIECE_LENGTH, HK)
    group_width = HK // N_TENSOR
    summed = jnp.zeros((PIECE_LENGTH, HIDDEN_DIMENSION), jnp.float32)
    for group_index in range(N_TENSOR):
        lower_col = group_index * group_width
        partial_term = jnp.dot(rounded[:, lower_col:lower_col + group_width], final_projection[lower_col:lower_col + group_width], preferred_element_type=jnp.float32)
        summed = summed + lax.optimization_barrier(partial_term.astype(jnp.bfloat16)).astype(jnp.float32)
    result = (widened + summed).astype(jnp.bfloat16)
    if write:
        trailing_keys = mapped_keys[PIECE_LENGTH - MEM:]
        tail_values = values[PIECE_LENGTH - MEM:]
        tail_read = readout[PIECE_LENGTH - MEM:]
        write_gate = jax.nn.sigmoid(jnp.dot(normed[PIECE_LENGTH - MEM:], write_gate_projection, preferred_element_type=jnp.float32))
        memory_update = (tail_values - tail_read) * write_gate[:, :, None]
        memory_matrix = memory_matrix + jnp.einsum('nxz,nxa->xza', trailing_keys, memory_update, precision=lax.Precision.HIGHEST)
        denominator_vectors = denominator_vectors + lax.optimization_barrier(jnp.sum(trailing_keys, axis=0))
    return (result, memory_matrix, denominator_vectors)

def reference(initial_stack_inputs, initial_sequence_starts, arriving_pieces, recall_embeddings, rescaling_factors, lookup_projection, content_projection, write_gate_projection, final_projection, associative_stores, denominator_vectors):
    carried_recurrence = initial_stack_inputs.reshape(DEPTH_TOTAL, PIECE_LENGTH, HIDDEN_DIMENSION)
    sequence_begin_flags = initial_sequence_starts
    for wave_step in range(STEPS):
        if wave_step > 0:
            arriving = jnp.concatenate([arriving_pieces[(wave_step - 1) * SEG:wave_step * SEG], recall_embeddings], axis=0)
            carried_recurrence = jnp.concatenate([arriving[None], carried_recurrence[:-1]], axis=0)
            sequence_begin_flags = jnp.concatenate([jnp.zeros((1,), jnp.int32), sequence_begin_flags[:-1].astype(jnp.int32)], axis=0)
        write = wave_step + 1 < STEPS
        carried_recurrence, associative_stores, denominator_vectors = lax.map(lambda inputs: section_layer(inputs, write), (carried_recurrence, sequence_begin_flags, rescaling_factors, lookup_projection, content_projection, write_gate_projection, final_projection, associative_stores, denominator_vectors))
    return carried_recurrence.reshape(DEPTH_TOTAL * PIECE_LENGTH, HIDDEN_DIMENSION)
```

```python
import functools

import jax
import jax.numpy as jnp
from jax import lax
from jax.experimental import pallas as pl
from jax.experimental.pallas import tpu as pltpu
from jax.sharding import Mesh
from jax.sharding import PartitionSpec as P

SEG = 128
MEM = 64
EPS = 1e-05
AXES = ("y_lo", "z", "x", "y_hi", "core")
SECTION = ("y_lo", "z")
TENSOR = ("x", "y_hi", "core")
CHIPS = ("x", "y_hi")
N_CHIPS = 8
BLOCK = 512
HEADS = 2
HD = 128
WIDE = HEADS * HD
SIDE = 128
HALF = 2 * WIDE + SIDE
HIDDEN = 8192
VMEM_LIMIT = 48 * 2**20
HIGHEST = lax.Precision.HIGHEST


def swap(value, axis):
    return lax.ppermute(value, axis, [(0, 1), (1, 0)])


def next_section(value, steps=1):
    return lax.ppermute(value, SECTION, [(i, i + steps) for i in range(16 - steps)])


def pick_kernel(core_ref, k_ref, v_ref, f_ref, w_out, f_out):
    w_out[0, :, :WIDE] = k_ref[0]
    w_out[0, :, WIDE:] = v_ref[0]
    f_out[...] = f_ref[...]


def pick(core, wk, wv, f):
    def theirs(b, core_ref):
        return (2 * b + 1 - core_ref[0], 0, 0)

    return pl.pallas_call(
        pick_kernel,
        grid_spec=pltpu.PrefetchScalarGridSpec(
            num_scalar_prefetch=1,
            grid=(N_CHIPS,),
            in_specs=[
                pl.BlockSpec((1, BLOCK, WIDE), theirs),
                pl.BlockSpec((1, BLOCK, WIDE), theirs),
                pl.BlockSpec((WIDE, BLOCK), lambda b, core_ref: (0, 2 * b + 1 - core_ref[0])),
            ],
            out_specs=[
                pl.BlockSpec((1, BLOCK, 2 * WIDE), lambda b, core_ref: (b, 0, 0)),
                pl.BlockSpec((WIDE, BLOCK), lambda b, core_ref: (0, b)),
            ],
        ),
        out_shape=[
            jax.ShapeDtypeStruct((N_CHIPS, BLOCK, 2 * WIDE), jnp.bfloat16),
            jax.ShapeDtypeStruct((WIDE, N_CHIPS * BLOCK), jnp.bfloat16),
        ],
        compiler_params=pltpu.CompilerParams(vmem_limit_bytes=16 * 2**20),
        cost_estimate=pl.CostEstimate(flops=0, bytes_accessed=12 * 2**20, transcendentals=0),
    )(core, wk, wv, f)


def project_kernel(
    write, core_ref, x_ref, gain_ref, k_ref, v_ref, got_ref, gate_ref, theirs_ref, mine_out, other_out
):
    core = core_ref[0]
    rows = x_ref.shape[1]
    dot = functools.partial(jnp.dot, preferred_element_type=jnp.float32)
    turned = functools.partial(
        lax.dot_general,
        dimension_numbers=(((1,), (1,)), ((), ())),
        preferred_element_type=jnp.float32,
    )
    k, v, other, squares, gate, theirs = 0.0, 0.0, 0.0, 0.0, 0.0, 0.0
    for b in range(N_CHIPS):
        wide = x_ref[b].astype(jnp.float32)
        squares += wide * wide
        scaled = (wide * gain_ref[b]).astype(jnp.bfloat16)
        k += dot(scaled, k_ref[2 * b + core])
        v += dot(scaled, v_ref[2 * b + core])
        other += dot(scaled, got_ref[b])
        if write:
            gate += turned(scaled[rows - MEM :], gate_ref[b])
            theirs += turned(scaled[rows - MEM :], theirs_ref[b])
    squares = jnp.sum(squares, axis=1, keepdims=True)
    mine_out[:, :WIDE] = k
    mine_out[:, WIDE : 2 * WIDE] = v
    other_out[:, : 2 * WIDE] = other
    lane = lax.broadcasted_iota(jnp.int32, (rows, SIDE), 1)
    side = jnp.where(lane == HEADS, squares, 0.0)
    mine_out[:, 2 * WIDE :] = side
    other_out[:, 2 * WIDE :] = side
    if write:
        mine_out[rows - MEM :, 2 * WIDE :] = side[rows - MEM :] + gate
        other_out[rows - MEM :, 2 * WIDE :] = side[rows - MEM :] + theirs


def project(core, x, gain, wk, wv, got, gate, theirs, write):
    rows = x.shape[1]
    out = jax.ShapeDtypeStruct((rows, HALF), jnp.float32)
    vmem = pl.BlockSpec(memory_space=pltpu.VMEM)
    return pl.pallas_call(
        functools.partial(project_kernel, write),
        in_specs=[pl.BlockSpec(memory_space=pltpu.SMEM)] + [vmem] * 7,
        out_specs=[vmem] * 2,
        out_shape=[out, out],
        compiler_params=pltpu.CompilerParams(vmem_limit_bytes=VMEM_LIMIT),
        cost_estimate=pl.CostEstimate(
            flops=2 * rows * 4096 * 1280, bytes_accessed=12 * 2**20, transcendentals=0
        ),
    )(core, x, gain, wk, wv, got, gate, theirs)


def memory_kernel(write, mine_ref, got_ref, keep_ref, a_ref, z_ref, read_ref, a_out, z_out):
    both = mine_ref[...] + got_ref[...]
    rows = both.shape[0]
    side = both[:, 2 * WIDE :]
    scale = lax.rsqrt(side[:, HEADS : HEADS + 1] * (1.0 / HIDDEN) + EPS)
    keep = keep_ref[0, 0]
    for h in range(HEADS):
        a = a_ref[h] * keep
        z = z_ref[h : h + 1] * keep
        k = both[:, h * HD : (h + 1) * HD] * scale
        k = jnp.where(k > 0, k + 1.0, jnp.exp(jnp.minimum(k, 0.0)))
        v = both[:, WIDE + h * HD : WIDE + (h + 1) * HD] * scale
        top = jnp.dot(k, a, precision=HIGHEST, preferred_element_type=jnp.float32)
        bottom = jnp.sum(k * z, axis=1, keepdims=True) + 1.0
        read = top / bottom
        read_ref[:, h * HD : (h + 1) * HD] = read.astype(jnp.bfloat16)
        if write:
            logit = side[rows - MEM :, h : h + 1] * scale[rows - MEM :]
            gate = 1.0 / (1.0 + jnp.exp(-logit))
            change = (v[rows - MEM :] - read[rows - MEM :]) * gate
            tail = k[rows - MEM :]
            a_out[h] = a + lax.dot_general(
                tail,
                change,
                (((0,), (0,)), ((), ())),
                precision=HIGHEST,
                preferred_element_type=jnp.float32,
            )
            z_out[h : h + 1] = z + jnp.sum(tail, axis=0, keepdims=True)
        else:
            a_out[h] = a
            z_out[h : h + 1] = z


def memory(mine, got, keep, a, z, write):
    rows = mine.shape[0]
    vmem = pl.BlockSpec(memory_space=pltpu.VMEM)
    return pl.pallas_call(
        functools.partial(memory_kernel, write),
        in_specs=[vmem, vmem, pl.BlockSpec(memory_space=pltpu.SMEM), vmem, vmem],
        out_specs=[vmem] * 3,
        out_shape=[
            jax.ShapeDtypeStruct((rows, WIDE), jnp.bfloat16),
            jax.ShapeDtypeStruct(a.shape, a.dtype),
            jax.ShapeDtypeStruct(z.shape, z.dtype),
        ],
        compiler_params=pltpu.CompilerParams(vmem_limit_bytes=16 * 2**20),
        cost_estimate=pl.CostEstimate(
            flops=2 * rows * WIDE * HD * 6, bytes_accessed=rows * HALF * 8, transcendentals=0
        ),
    )(mine, got, keep, a, z)


def output_kernel(core_ref, near_ref, far_ref, f_ref, got_ref, p_ref):
    core = core_ref[0]
    near, far = near_ref[...], far_ref[...]
    for b in range(N_CHIPS):
        columns = pl.ds(pl.multiple_of((2 * b + core) * BLOCK, BLOCK), BLOCK)
        part = jnp.dot(near, f_ref[:, columns], preferred_element_type=jnp.float32)
        part += jnp.dot(
            far, got_ref[:, b * BLOCK : (b + 1) * BLOCK], preferred_element_type=jnp.float32
        )
        p_ref[b] = part.astype(jnp.bfloat16)


def output(core, near, far, f, got):
    rows = near.shape[0]
    vmem = pl.BlockSpec(memory_space=pltpu.VMEM)
    return pl.pallas_call(
        output_kernel,
        in_specs=[pl.BlockSpec(memory_space=pltpu.SMEM)] + [vmem] * 4,
        out_specs=vmem,
        out_shape=jax.ShapeDtypeStruct((N_CHIPS, rows, BLOCK), jnp.bfloat16),
        compiler_params=pltpu.CompilerParams(vmem_limit_bytes=VMEM_LIMIT),
        cost_estimate=pl.CostEstimate(
            flops=2 * rows * 2 * WIDE * 4096, bytes_accessed=4096 * 2 * WIDE * 2, transcendentals=0
        ),
    )(core, near, far, f, got)


def gather_chips(x):
    return lax.all_to_all(
        jnp.broadcast_to(x[None], (N_CHIPS,) + x.shape), CHIPS, 0, 0, tiled=True
    )


def scatter_chips(p, x):
    parts = lax.all_to_all(p, CHIPS, 0, 0, tiled=True)
    total = jnp.sum(parts.astype(jnp.float32), axis=0)
    return (x.astype(jnp.float32) + total).astype(jnp.bfloat16)


def local(
    initial_stack_inputs,
    initial_sequence_starts,
    arriving_pieces,
    recall_embeddings,
    rescaling_factors,
    lookup_projection,
    content_projection,
    write_gate_projection,
    final_projection,
    associative_stores,
    denominator_vectors,
):
    core = lax.axis_index("core")
    which = core.astype(jnp.int32).reshape(1)
    section_zero = (lax.axis_index("y_lo") == 0) & (lax.axis_index("z") == 0)
    steps = arriving_pieces.shape[0] // SEG + 1

    x = initial_stack_inputs
    gathered = gather_chips(x)
    flags = [initial_sequence_starts]
    for t in range(1, steps):
        flags.append(next_section(initial_sequence_starts, t))

    wk = lookup_projection[0].reshape(2 * N_CHIPS, BLOCK, WIDE)
    wv = content_projection[0].reshape(2 * N_CHIPS, BLOCK, WIDE)
    f = final_projection[0]
    w_sent, f_sent = pick(which, wk, wv, f)
    w_got = swap(w_sent, "core")
    f_got = swap(f_sent, "core")
    gain = lax.dynamic_index_in_dim(
        rescaling_factors.reshape(N_CHIPS, 2, 1, BLOCK), core, 1, keepdims=False
    )
    gates = write_gate_projection[0].T.reshape(HEADS, N_CHIPS, 2, BLOCK).transpose(2, 1, 0, 3)
    fill = ((0, 0), (0, SIDE - HEADS), (0, 0))
    gate = jnp.pad(lax.dynamic_index_in_dim(gates, core, 0, keepdims=False), fill)
    theirs = swap(lax.dynamic_index_in_dim(gates, 1 - core, 0, keepdims=False), "core")
    theirs = jnp.pad(theirs, fill)

    a = associative_stores[0]
    z = denominator_vectors[0]
    a, flags = lax.optimization_barrier((a, flags))
    for t in range(steps):
        write = t + 1 < steps
        if t > 0:
            moved = next_section(x)
            entering = jnp.concatenate(
                [arriving_pieces[(t - 1) * SEG : t * SEG], recall_embeddings], axis=0
            )
            x = jnp.where(section_zero, entering, moved)
            gathered = gather_chips(x)
        keep = (1 - flags[t]).astype(jnp.float32).reshape(1, 1)
        mine, other = project(which, gathered, gain, wk, wv, w_got, gate, theirs, write)
        read, a, z = memory(mine, swap(other, "core"), keep, a, z, write)
        p = output(which, read, swap(read, "core"), f, f_got)
        x = scatter_chips(p, x)
    return x


def solution(mesh):
    fine = Mesh(mesh.devices.reshape(2, 8, 4, 2, 2), AXES)
    return jax.shard_map(
        local,
        mesh=fine,
        in_specs=(
            P(SECTION, TENSOR),
            P(SECTION),
            P(None, TENSOR),
            P(None, TENSOR),
            P(SECTION, None),
            P(SECTION, None, TENSOR),
            P(SECTION, None, TENSOR),
            P(SECTION, None, TENSOR),
            P(SECTION, TENSOR, None),
            P(SECTION, TENSOR, None, None),
            P(SECTION, TENSOR, None),
        ),
        out_specs=P(SECTION, TENSOR),
        check_vma=False,
    )
```

```python
import functools

import jax
import jax.numpy as jnp
from jax import lax
from jax.experimental import pallas as pl
from jax.experimental.pallas import tpu as pltpu
from jax.sharding import Mesh
from jax.sharding import PartitionSpec as P

SEG = 128
PIECE = 192
MEM = 64
EPS = 1e-05
AXES = ("y_lo", "z", "x", "y_hi", "core")
SECTION = ("y_lo", "z")
TENSOR = ("x", "y_hi", "core")
CHIPS = ("x", "y_hi")
N_CHIPS = 8
FLAG_ROWS = 16
PARTS = 4
BLOCK = 512
HEADS = 2
HD = 128
WIDE = HEADS * HD
SIDE = 128
HALF = 2 * WIDE + SIDE
HIDDEN = 8192
VMEM_LIMIT = 14 * 2**20
HIGHEST = lax.Precision.HIGHEST


VMEM = pl.BlockSpec(memory_space=pltpu.VMEM)
SMEM = pl.BlockSpec(memory_space=pltpu.SMEM)


def swap(value, axis):
    return lax.ppermute(value, axis, [(0, 1), (1, 0)])


def next_section(value):
    return lax.ppermute(value, SECTION, [(i, i + 1) for i in range(15)])


def pick_kernel(core_ref, k_ref, v_ref, f_ref, w_keep, w_sent, f_keep, f_sent):
    core = core_ref[0]
    w_keep[0, :, :WIDE] = k_ref[core]
    w_keep[0, :, WIDE:] = v_ref[core]
    w_sent[0, :, :WIDE] = k_ref[1 - core]
    w_sent[0, :, WIDE:] = v_ref[1 - core]
    f_keep[0] = f_ref[:, pl.ds(pl.multiple_of(core * BLOCK, BLOCK), BLOCK)]
    f_sent[0] = f_ref[:, pl.ds(pl.multiple_of((1 - core) * BLOCK, BLOCK), BLOCK)]


def pick(core, wk, wv, f, part):
    count = N_CHIPS // PARTS
    pair = pl.BlockSpec((2, BLOCK, WIDE), lambda b: (part * count + b, 0, 0))
    w_block = pl.BlockSpec((1, BLOCK, 2 * WIDE), lambda b: (b, 0, 0))
    f_block = pl.BlockSpec((1, WIDE, BLOCK), lambda b: (b, 0, 0))
    w_shape = jax.ShapeDtypeStruct((count, BLOCK, 2 * WIDE), jnp.bfloat16)
    f_shape = jax.ShapeDtypeStruct((count, WIDE, BLOCK), jnp.bfloat16)
    return pl.pallas_call(
        pick_kernel,
        grid=(count,),
        in_specs=[SMEM, pair, pair, pl.BlockSpec((WIDE, 2 * BLOCK), lambda b: (0, part * count + b))],
        out_specs=[w_block, w_block, f_block, f_block],
        out_shape=[w_shape, w_shape, f_shape, f_shape],
        compiler_params=pltpu.CompilerParams(vmem_limit_bytes=VMEM_LIMIT),
        cost_estimate=pl.CostEstimate(flops=0, bytes_accessed=0, transcendentals=0),
    )(core, wk, wv, f)


def project_kernel(write, x_ref, gain_ref, gate_ref, *refs):
    keep_refs, got_refs, (mine_out, other_out) = refs[:PARTS], refs[PARTS : 2 * PARTS], refs[-2:]
    rows = x_ref.shape[1]
    dot = functools.partial(jnp.dot, preferred_element_type=jnp.float32)
    squares, gate, mine, other = 0.0, 0.0, 0.0, 0.0
    for b in range(N_CHIPS):
        part, at = divmod(b, N_CHIPS // PARTS)
        wide = x_ref[b].astype(jnp.float32)
        squares += wide * wide
        scaled = (wide * gain_ref[b]).astype(jnp.bfloat16)
        mine += dot(scaled, keep_refs[part][at])
        other += dot(scaled, got_refs[part][at])
        if write:
            gate += dot(scaled[rows - MEM :], gate_ref[b])
    squares = jnp.sum(squares, axis=1, keepdims=True)
    lane = lax.broadcasted_iota(jnp.int32, (rows, SIDE), 1)
    side = jnp.where(lane == 2 * HEADS, squares, 0.0)
    mine_out[:, : 2 * WIDE] = mine
    other_out[:, : 2 * WIDE] = other
    mine_out[:, 2 * WIDE :] = side
    other_out[:, 2 * WIDE :] = side
    if write:
        mine_out[rows - MEM :, 2 * WIDE :] = side[rows - MEM :] + gate
        other_out[rows - MEM :, 2 * WIDE :] = side[rows - MEM :] + gate


def project(x, gain, gate, keep, got, write):
    rows = x.shape[1]
    out = jax.ShapeDtypeStruct((rows, HALF), jnp.float32)
    return pl.pallas_call(
        functools.partial(project_kernel, write),
        in_specs=[VMEM] * (3 + 2 * PARTS),
        out_specs=[VMEM] * 2,
        out_shape=[out, out],
        compiler_params=pltpu.CompilerParams(vmem_limit_bytes=VMEM_LIMIT),
        cost_estimate=pl.CostEstimate(
            flops=2 * rows * 4096 * 1024, bytes_accessed=0, transcendentals=0
        ),
    )(x, gain, gate, *keep, *got)


def memory_kernel(write, mine_ref, got_ref, keep_ref, a_ref, z_ref, read_ref, *state):
    both = mine_ref[:, : 2 * WIDE] + got_ref[:, : 2 * WIDE]
    rows = both.shape[0]
    side, got_side = mine_ref[:, 2 * WIDE :], got_ref[:, 2 * WIDE :]
    total = side[:, 2 * HEADS : 2 * HEADS + 1] + got_side[:, 2 * HEADS : 2 * HEADS + 1]
    scale = lax.rsqrt(total * (1.0 / HIDDEN) + EPS)
    keep = keep_ref[0, 0]
    for h in range(HEADS):
        a = a_ref[h] * keep
        z = z_ref[h : h + 1] * keep
        k = both[:, h * HD : (h + 1) * HD] * scale
        k = jnp.where(k > 0, k + 1.0, jnp.exp(jnp.minimum(k, 0.0)))
        v = both[:, WIDE + h * HD : WIDE + (h + 1) * HD] * scale
        top = jnp.dot(k, a, precision=HIGHEST, preferred_element_type=jnp.float32)
        bottom = jnp.sum(k * z, axis=1, keepdims=True) + 1.0
        read = top / bottom
        read_ref[:, h * HD : (h + 1) * HD] = read.astype(jnp.bfloat16)
        if write:
            logit = side[rows - MEM :, h : h + 1] + got_side[rows - MEM :, HEADS + h : HEADS + h + 1]
            logit = logit * scale[rows - MEM :]
            gate = 1.0 / (1.0 + jnp.exp(-logit))
            change = (v[rows - MEM :] - read[rows - MEM :]) * gate
            tail = k[rows - MEM :]
            state[0][h] = a + lax.dot_general(
                tail,
                change,
                (((0,), (0,)), ((), ())),
                precision=HIGHEST,
                preferred_element_type=jnp.float32,
            )
            state[1][h : h + 1] = z + jnp.sum(tail, axis=0, keepdims=True)


def memory(mine, got, keep, a, z, write):
    rows = mine.shape[0]
    shapes = [jax.ShapeDtypeStruct((rows, WIDE), jnp.bfloat16)]
    if write:
        shapes += [jax.ShapeDtypeStruct(a.shape, a.dtype), jax.ShapeDtypeStruct(z.shape, z.dtype)]
    return pl.pallas_call(
        functools.partial(memory_kernel, write),
        in_specs=[VMEM, VMEM, SMEM, VMEM, VMEM],
        out_specs=[VMEM] * len(shapes),
        out_shape=shapes,
        compiler_params=pltpu.CompilerParams(vmem_limit_bytes=16 * 2**20),
        cost_estimate=pl.CostEstimate(
            flops=2 * rows * WIDE * HD * 6, bytes_accessed=rows * HALF * 8, transcendentals=0
        ),
    )(mine, got, keep, a, z)


def output_kernel(near_ref, far_ref, *refs):
    keep_refs, got_refs, p_ref = refs[:PARTS], refs[PARTS : 2 * PARTS], refs[-1]
    near, far = near_ref[...], far_ref[...]
    for b in range(N_CHIPS):
        i, at = divmod(b, N_CHIPS // PARTS)
        part = jnp.dot(near, keep_refs[i][at], preferred_element_type=jnp.float32)
        part += jnp.dot(far, got_refs[i][at], preferred_element_type=jnp.float32)
        p_ref[b] = part.astype(jnp.bfloat16)


def output(near, far, keep, got):
    rows = near.shape[0]
    return pl.pallas_call(
        output_kernel,
        in_specs=[VMEM] * (2 + 2 * PARTS),
        out_specs=VMEM,
        out_shape=jax.ShapeDtypeStruct((N_CHIPS, rows, BLOCK), jnp.bfloat16),
        compiler_params=pltpu.CompilerParams(vmem_limit_bytes=VMEM_LIMIT),
        cost_estimate=pl.CostEstimate(
            flops=2 * rows * 2 * WIDE * 4096, bytes_accessed=0, transcendentals=0
        ),
    )(near, far, *keep, *got)


def copies(x):
    return jnp.broadcast_to(x[None], (N_CHIPS,) + x.shape)


def exchange(blocks):
    return lax.all_to_all(blocks, CHIPS, 0, 0, tiled=True)


def local(
    initial_stack_inputs,
    initial_sequence_starts,
    arriving_pieces,
    recall_embeddings,
    rescaling_factors,
    lookup_projection,
    content_projection,
    write_gate_projection,
    final_projection,
    associative_stores,
    denominator_vectors,
):
    core = lax.axis_index("core")
    which = core.astype(jnp.int32).reshape(1)
    section_zero = (lax.axis_index("y_lo") == 0) & (lax.axis_index("z") == 0)
    steps = arriving_pieces.shape[0] // SEG + 1

    x = initial_stack_inputs
    outgoing, which = lax.optimization_barrier((copies(x), which))
    flag = (initial_sequence_starts[0] > 0).astype(jnp.bfloat16)

    wk = lookup_projection[0].reshape(2 * N_CHIPS, BLOCK, WIDE)
    wv = content_projection[0].reshape(2 * N_CHIPS, BLOCK, WIDE)
    picked = [pick(which, wk, wv, final_projection[0], part) for part in range(PARTS)]
    w_keep, w_sent, f_keep, f_sent = zip(*picked)
    w_got = [swap(w, "core") for w in w_sent]
    f_got = [swap(f, "core") for f in f_sent]
    gain = lax.dynamic_index_in_dim(
        rescaling_factors.reshape(N_CHIPS, 2, 1, BLOCK), core, 1, keepdims=False
    )
    gates = write_gate_projection[0].T.reshape(HEADS, N_CHIPS, 2, BLOCK)
    gate = lax.dynamic_index_in_dim(gates, core, 2, keepdims=False)
    theirs = swap(lax.dynamic_index_in_dim(gates, 1 - core, 2, keepdims=False), "core")
    gate = jnp.concatenate([gate, theirs], axis=0).transpose(1, 2, 0)
    gate = jnp.pad(gate, ((0, 0), (0, 0), (0, SIDE - 2 * HEADS)))

    a = associative_stores[0]
    z = denominator_vectors[0]
    for t in range(steps):
        write = t + 1 < steps
        if t > 0:
            sent = jnp.concatenate([x, jnp.broadcast_to(flag, (FLAG_ROWS, BLOCK))], axis=0)
            moved = next_section(sent)
            entering = jnp.concatenate(
                [arriving_pieces[(t - 1) * SEG : t * SEG], recall_embeddings], axis=0
            )
            x = jnp.where(section_zero, entering, moved[:PIECE])
            flag = jnp.where(section_zero, jnp.zeros((), jnp.bfloat16), moved[PIECE, 0])
            outgoing = copies(x)
        keep = (1.0 - flag.astype(jnp.float32)).reshape(1, 1)
        mine, other = project(exchange(outgoing), gain, gate, w_keep, w_got, write)
        read, *state = memory(mine, swap(other, "core"), keep, a, z, write)
        if write:
            a, z = state
        p = exchange(output(read, swap(read, "core"), f_keep, f_got))
        total = jnp.sum(p.astype(jnp.float32), axis=0)
        x = (x.astype(jnp.float32) + total).astype(jnp.bfloat16)
    return x


def solution(mesh):
    fine = Mesh(mesh.devices.reshape(2, 8, 4, 2, 2), AXES)
    return jax.shard_map(
        local,
        mesh=fine,
        in_specs=(
            P(SECTION, TENSOR),
            P(SECTION),
            P(None, TENSOR),
            P(None, TENSOR),
            P(SECTION, None),
            P(SECTION, None, TENSOR),
            P(SECTION, None, TENSOR),
            P(SECTION, None, TENSOR),
            P(SECTION, TENSOR, None),
            P(SECTION, TENSOR, None, None),
            P(SECTION, TENSOR, None),
        ),
        out_specs=P(SECTION, TENSOR),
        check_vma=False,
    )
```

```python
import functools

import jax
import jax.numpy as jnp
from jax import lax
from jax.experimental import pallas as pl
from jax.experimental.pallas import tpu as pltpu
from jax.sharding import Mesh
from jax.sharding import PartitionSpec as P

SEG = 128
PIECE = 192
MEM = 64
EPS = 1e-05
AXES = ("y_lo", "z", "x", "y_hi", "core")
SECTION = ("y_lo", "z")
TENSOR = ("x", "y_hi", "core")
CHIPS = ("x", "y_hi")
N_CHIPS = 8
FLAG_ROWS = 16
BLOCK = 512
HEADS = 2
SIDE = 128
GATE_ROWS = 16
HD = 128
WIDE = HEADS * HD
HIDDEN = 8192
VMEM_LIMIT = 48 * 2**20
HIGHEST = lax.Precision.HIGHEST


VMEM = pl.BlockSpec(memory_space=pltpu.VMEM)
SMEM = pl.BlockSpec(memory_space=pltpu.SMEM)


def swap(value, axis):
    return lax.ppermute(value, axis, [(0, 1), (1, 0)])


def next_section(value):
    return lax.ppermute(value, SECTION, [(i, i + 1) for i in range(15)])


ANY = pl.BlockSpec(memory_space=pl.ANY)


def pick_kernel(core_ref, f_ref, keep_ref, sent_ref):
    core = core_ref[0]
    keep_ref[0] = f_ref[:, pl.ds(pl.multiple_of(core * BLOCK, BLOCK), BLOCK)]
    sent_ref[0] = f_ref[:, pl.ds(pl.multiple_of((1 - core) * BLOCK, BLOCK), BLOCK)]


def pick(core, f):
    block = pl.BlockSpec((1, WIDE, BLOCK), lambda b: (b, 0, 0))
    shape = jax.ShapeDtypeStruct((N_CHIPS, WIDE, BLOCK), jnp.bfloat16)
    return pl.pallas_call(
        pick_kernel,
        grid=(N_CHIPS,),
        in_specs=[SMEM, pl.BlockSpec((WIDE, 2 * BLOCK), lambda b: (0, b))],
        out_specs=[block, block],
        out_shape=[shape, shape],
        compiler_params=pltpu.CompilerParams(vmem_limit_bytes=VMEM_LIMIT),
        cost_estimate=pl.CostEstimate(flops=0, bytes_accessed=0, transcendentals=0),
    )(core, f)


def project_half(write, offset, x_ref, gain_ref, wk_ref, wv_ref, gate_ref, bufs, sems):
    x_buf, k_buf, v_buf = bufs
    rows = x_ref.shape[1]
    copies = []
    for b in range(N_CHIPS):
        place = 2 * b + offset
        group = []
        for i, (source, target) in enumerate(
            (
                (x_ref.at[b], x_buf.at[b]),
                (wk_ref.at[place], k_buf.at[b]),
                (wv_ref.at[place], v_buf.at[b]),
            )
        ):
            copy = pltpu.make_async_copy(source, target, sems.at[i, b])
            copy.start()
            group.append(copy)
        copies.append(group)
    dot = functools.partial(jnp.dot, preferred_element_type=jnp.float32)
    squares, gates, keys, values = 0.0, 0.0, 0.0, 0.0
    for b in range(N_CHIPS):
        place = 2 * b + offset
        for copy in copies[b]:
            copy.wait()
        wide = x_buf[b].astype(jnp.float32)
        squares += wide * wide
        scaled = (wide * gain_ref[place]).astype(jnp.bfloat16)
        keys += dot(scaled, k_buf[b])
        values += dot(scaled, v_buf[b])
        if write:
            gates += lax.dot_general(
                scaled[rows - MEM :],
                gate_ref[place],
                (((1,), (1,)), ((), ())),
                preferred_element_type=jnp.float32,
            )
    return keys, values, jnp.sum(squares, axis=1, keepdims=True), gates


def first_kernel(write, core_ref, x_ref, gain_ref, wk_ref, wv_ref, gate_ref, sum_ref, *rest):
    *bufs, sems = rest
    rows = x_ref.shape[1]
    keys, values, squares, gates = project_half(
        write, core_ref[0], x_ref, gain_ref, wk_ref, wv_ref, gate_ref, bufs, sems
    )
    sum_ref[:, :WIDE] = keys
    sum_ref[:, WIDE : 2 * WIDE] = values
    lane = lax.broadcasted_iota(jnp.int32, (rows, SIDE), 1)
    side = jnp.where(lane == GATE_ROWS, squares, 0.0)
    sum_ref[:, 2 * WIDE :] = side
    if write:
        sum_ref[rows - MEM :, 2 * WIDE : 2 * WIDE + GATE_ROWS] = gates


def read_kernel(
    write, core_ref, keep_ref, sum_ref, x_ref, gain_ref, wk_ref, wv_ref, gate_ref, a_ref, z_ref,
    read_ref, *rest,
):
    *state, x_buf, k_buf, v_buf, sems = rest
    rows = x_ref.shape[1]
    keys, values, squares, gates = project_half(
        write, 1 - core_ref[0], x_ref, gain_ref, wk_ref, wv_ref, gate_ref,
        (x_buf, k_buf, v_buf), sems,
    )
    keys += sum_ref[:, :WIDE]
    values += sum_ref[:, WIDE : 2 * WIDE]
    side = sum_ref[:, 2 * WIDE :]
    squares += side[:, GATE_ROWS : GATE_ROWS + 1]
    scale = lax.rsqrt(squares * (1.0 / HIDDEN) + EPS)
    keep = keep_ref[0, 0]
    for h in range(HEADS):
        a = a_ref[h] * keep
        z = z_ref[h : h + 1] * keep
        k = keys[:, h * HD : (h + 1) * HD] * scale
        k = jnp.where(k > 0, k + 1.0, jnp.exp(jnp.minimum(k, 0.0)))
        top = jnp.dot(k, a, precision=HIGHEST, preferred_element_type=jnp.float32)
        bottom = jnp.sum(k * z, axis=1, keepdims=True) + 1.0
        read = top / bottom
        read_ref[:, h * HD : (h + 1) * HD] = read.astype(jnp.bfloat16)
        if write:
            v = values[rows - MEM :, h * HD : (h + 1) * HD] * scale[rows - MEM :]
            logit = (side[rows - MEM :, h : h + 1] + gates[:, h : h + 1]) * scale[rows - MEM :]
            gate = 1.0 / (1.0 + jnp.exp(-logit))
            tail = k[rows - MEM :]
            state[0][h] = a + lax.dot_general(
                tail,
                (v - read[rows - MEM :]) * gate,
                (((0,), (0,)), ((), ())),
                precision=HIGHEST,
                preferred_element_type=jnp.float32,
            )
            state[1][h : h + 1] = z + jnp.sum(tail, axis=0, keepdims=True)


def half_scratch(rows):
    weights = pltpu.VMEM((N_CHIPS, BLOCK, WIDE), jnp.bfloat16)
    x = pltpu.VMEM((N_CHIPS, rows, BLOCK), jnp.bfloat16)
    return [x, weights, weights, pltpu.SemaphoreType.DMA((3, N_CHIPS))]


def project_first(core, own, gain, wk, wv, gate, write):
    rows = own.shape[1]
    return pl.pallas_call(
        functools.partial(first_kernel, write),
        in_specs=[SMEM, ANY, VMEM, ANY, ANY, VMEM],
        out_specs=VMEM,
        out_shape=jax.ShapeDtypeStruct((rows, 2 * WIDE + SIDE), jnp.float32),
        scratch_shapes=half_scratch(rows),
        compiler_params=pltpu.CompilerParams(vmem_limit_bytes=VMEM_LIMIT),
        cost_estimate=pl.CostEstimate(
            flops=rows * HIDDEN * 2 * WIDE, bytes_accessed=6 * 2**20, transcendentals=0
        ),
    )(core, own, gain, wk, wv, gate)


def read_memory(core, keep, begun, got, gain, wk, wv, gate, a, z, write):
    rows = got.shape[1]
    shapes = [jax.ShapeDtypeStruct((rows, WIDE), jnp.bfloat16)]
    if write:
        shapes += [jax.ShapeDtypeStruct(a.shape, a.dtype), jax.ShapeDtypeStruct(z.shape, z.dtype)]
    return pl.pallas_call(
        functools.partial(read_kernel, write),
        in_specs=[SMEM, SMEM, VMEM, ANY, VMEM, ANY, ANY, VMEM, VMEM, VMEM],
        out_specs=[VMEM] * len(shapes),
        out_shape=shapes,
        scratch_shapes=half_scratch(rows),
        compiler_params=pltpu.CompilerParams(vmem_limit_bytes=VMEM_LIMIT),
        cost_estimate=pl.CostEstimate(
            flops=rows * HIDDEN * 2 * WIDE, bytes_accessed=6 * 2**20, transcendentals=0
        ),
    )(core, keep, begun, got, gain, wk, wv, gate, a, z)


def output_kernel(near_ref, far_ref, keep_ref, got_ref, p_ref, got_buf, sems):
    copies = []
    for b in range(N_CHIPS):
        copies.append(pltpu.make_async_copy(got_ref.at[b], got_buf.at[b], sems.at[b]))
        copies[-1].start()
    near, far = near_ref[...], far_ref[...]
    for b in range(N_CHIPS):
        part = jnp.dot(near, keep_ref[b], preferred_element_type=jnp.float32)
        copies[b].wait()
        part += jnp.dot(far, got_buf[b], preferred_element_type=jnp.float32)
        p_ref[b] = part.astype(jnp.bfloat16)


def output(near, far, keep, got):
    rows = near.shape[0]
    return pl.pallas_call(
        output_kernel,
        in_specs=[VMEM, VMEM, VMEM, ANY],
        out_specs=VMEM,
        out_shape=jax.ShapeDtypeStruct((N_CHIPS, rows, BLOCK), jnp.bfloat16),
        scratch_shapes=[
            pltpu.VMEM((N_CHIPS, WIDE, BLOCK), jnp.bfloat16),
            pltpu.SemaphoreType.DMA((N_CHIPS,)),
        ],
        compiler_params=pltpu.CompilerParams(vmem_limit_bytes=VMEM_LIMIT),
        cost_estimate=pl.CostEstimate(
            flops=2 * rows * 2 * WIDE * 4096, bytes_accessed=2 * 2**20, transcendentals=0
        ),
    )(near, far, keep, got)


def copies(x):
    return jnp.broadcast_to(x[None], (N_CHIPS,) + x.shape)


def exchange(blocks):
    return lax.all_to_all(blocks, CHIPS, 0, 0, tiled=True)


def local(
    initial_stack_inputs,
    initial_sequence_starts,
    arriving_pieces,
    recall_embeddings,
    rescaling_factors,
    lookup_projection,
    content_projection,
    write_gate_projection,
    final_projection,
    associative_stores,
    denominator_vectors,
):
    core = lax.axis_index("core")
    which = core.astype(jnp.int32).reshape(1)
    section_zero = (lax.axis_index("y_lo") == 0) & (lax.axis_index("z") == 0)
    steps = arriving_pieces.shape[0] // SEG + 1

    x = initial_stack_inputs
    outgoing, which = lax.optimization_barrier((copies(x), which))
    flag = (initial_sequence_starts[0] > 0).astype(jnp.bfloat16)

    wk = lookup_projection[0].reshape(2 * N_CHIPS, BLOCK, WIDE)
    wv = content_projection[0].reshape(2 * N_CHIPS, BLOCK, WIDE)
    f_keep, f_sent = pick(which, final_projection[0])
    f_got = swap(f_sent, "core")
    gain = rescaling_factors.reshape(2 * N_CHIPS, 1, BLOCK)
    gate = write_gate_projection[0].T.reshape(HEADS, 2 * N_CHIPS, BLOCK).transpose(1, 0, 2)
    gate = jnp.pad(gate, ((0, 0), (0, GATE_ROWS - HEADS), (0, 0)))

    a = associative_stores[0]
    z = denominator_vectors[0]
    for t in range(steps):
        write = t + 1 < steps
        if t > 0:
            sent = jnp.concatenate([x, jnp.broadcast_to(flag, (FLAG_ROWS, BLOCK))], axis=0)
            moved = next_section(sent)
            entering = jnp.concatenate(
                [arriving_pieces[(t - 1) * SEG : t * SEG], recall_embeddings], axis=0
            )
            x = jnp.where(section_zero, entering, moved[:PIECE])
            flag = jnp.where(section_zero, jnp.zeros((), jnp.bfloat16), moved[PIECE, 0])
            outgoing = copies(x)
        keep = (1.0 - flag.astype(jnp.float32)).reshape(1, 1)
        own = exchange(outgoing)
        got = swap(own, "core")
        begun = project_first(which, own, gain, wk, wv, gate, write)
        read, *state = read_memory(which, keep, begun, got, gain, wk, wv, gate, a, z, write)
        if write:
            a, z = state
        p = exchange(output(read, swap(read, "core"), f_keep, f_got))
        total = jnp.sum(p.astype(jnp.float32), axis=0)
        x = (x.astype(jnp.float32) + total).astype(jnp.bfloat16)
    return x


def solution(mesh):
    fine = Mesh(mesh.devices.reshape(2, 8, 4, 2, 2), AXES)
    return jax.shard_map(
        local,
        mesh=fine,
        in_specs=(
            P(SECTION, TENSOR),
            P(SECTION),
            P(None, TENSOR),
            P(None, TENSOR),
            P(SECTION, None),
            P(SECTION, None, TENSOR),
            P(SECTION, None, TENSOR),
            P(SECTION, None, TENSOR),
            P(SECTION, TENSOR, None),
            P(SECTION, TENSOR, None, None),
            P(SECTION, TENSOR, None),
        ),
        out_specs=P(SECTION, TENSOR),
        check_vma=False,
    )
```

```python
import functools

import jax
import jax.numpy as jnp
from jax import lax
from jax.experimental import pallas as pl
from jax.experimental.pallas import tpu as pltpu
from jax.sharding import Mesh
from jax.sharding import PartitionSpec as P

SEG = 128
PIECE = 192
MEM = 64
EPS = 1e-05
AXES = ("y_lo", "z", "x", "y_hi", "core")
SECTION = ("y_lo", "z")
TENSOR = ("x", "y_hi", "core")
CHIPS = ("x", "y_hi")
N_CHIPS = 8
FLAG_ROWS = 16
BLOCK = 512
HEADS = 2
SIDE = 128
GATE_ROWS = 16
HD = 128
WIDE = HEADS * HD
HIDDEN = 8192
VMEM_LIMIT = 48 * 2**20
HIGHEST = lax.Precision.HIGHEST


VMEM = pl.BlockSpec(memory_space=pltpu.VMEM)
SMEM = pl.BlockSpec(memory_space=pltpu.SMEM)


def swap(value, axis):
    return lax.ppermute(value, axis, [(0, 1), (1, 0)])


def next_section(value):
    return lax.ppermute(value, SECTION, [(i, i + 1) for i in range(15)])


ANY = pl.BlockSpec(memory_space=pl.ANY)


def pick_kernel(core_ref, f_ref, keep_ref, sent_ref):
    core = core_ref[0]
    keep_ref[0] = f_ref[:, pl.ds(pl.multiple_of(core * BLOCK, BLOCK), BLOCK)]
    sent_ref[0] = f_ref[:, pl.ds(pl.multiple_of((1 - core) * BLOCK, BLOCK), BLOCK)]


def pick(core, f):
    block = pl.BlockSpec((1, WIDE, BLOCK), lambda b: (b, 0, 0))
    shape = jax.ShapeDtypeStruct((N_CHIPS, WIDE, BLOCK), jnp.bfloat16)
    return pl.pallas_call(
        pick_kernel,
        grid=(N_CHIPS,),
        in_specs=[SMEM, pl.BlockSpec((WIDE, 2 * BLOCK), lambda b: (0, b))],
        out_specs=[block, block],
        out_shape=[shape, shape],
        compiler_params=pltpu.CompilerParams(vmem_limit_bytes=VMEM_LIMIT),
        cost_estimate=pl.CostEstimate(flops=0, bytes_accessed=0, transcendentals=0),
    )(core, f)


def project_half(write, offset, x_ref, gain_ref, wk_ref, wv_ref, gate_ref, bufs, sems, extra=None):
    x_buf, k_buf, v_buf = bufs
    rows = x_ref.shape[1]
    copies = []
    for b in range(N_CHIPS):
        place = 2 * b + offset
        group = []
        for i, (source, target) in enumerate(
            (
                (x_ref.at[b], x_buf.at[b]),
                (wk_ref.at[place], k_buf.at[b]),
                (wv_ref.at[place], v_buf.at[b]),
            )
        ):
            copy = pltpu.make_async_copy(source, target, sems.at[i, b])
            copy.start()
            group.append(copy)
        copies.append(group)
    if extra is not None:
        extra.start()
    dot = functools.partial(jnp.dot, preferred_element_type=jnp.float32)
    squares, gates, keys, values = 0.0, 0.0, 0.0, 0.0
    for b in range(N_CHIPS):
        place = 2 * b + offset
        for copy in copies[b]:
            copy.wait()
        wide = x_buf[b].astype(jnp.float32)
        squares += wide * wide
        scaled = (wide * gain_ref[place]).astype(jnp.bfloat16)
        keys += dot(scaled, k_buf[b])
        values += dot(scaled, v_buf[b])
        if write:
            gates += lax.dot_general(
                scaled[rows - MEM :],
                gate_ref[place],
                (((1,), (1,)), ((), ())),
                preferred_element_type=jnp.float32,
            )
    return keys, values, jnp.sum(squares, axis=1, keepdims=True), gates


def first_kernel(write, core_ref, x_ref, gain_ref, wk_ref, wv_ref, gate_ref, sum_ref, *rest):
    *bufs, sems = rest
    rows = x_ref.shape[1]
    keys, values, squares, gates = project_half(
        write, core_ref[0], x_ref, gain_ref, wk_ref, wv_ref, gate_ref, bufs, sems
    )
    sum_ref[:, :WIDE] = keys
    sum_ref[:, WIDE : 2 * WIDE] = values
    lane = lax.broadcasted_iota(jnp.int32, (rows, SIDE), 1)
    side = jnp.where(lane == GATE_ROWS, squares, 0.0)
    sum_ref[:, 2 * WIDE :] = side
    if write:
        sum_ref[rows - MEM :, 2 * WIDE : 2 * WIDE + GATE_ROWS] = gates


def read_kernel(
    write, core_ref, entered_ref, sum_ref, x_ref, gain_ref, wk_ref, wv_ref, gate_ref, f_ref,
    a_ref, z_ref, read_ref, f_next, tile_ref, *rest,
):
    *state, x_buf, k_buf, v_buf, sems, f_sem = rest
    rows = x_ref.shape[1]
    f_copy = pltpu.make_async_copy(f_ref, f_next, f_sem.at[0])
    keys, values, squares, gates = project_half(
        write, 1 - core_ref[0], x_ref, gain_ref, wk_ref, wv_ref, gate_ref,
        (x_buf, k_buf, v_buf), sems, f_copy,
    )
    keys += sum_ref[:, :WIDE]
    values += sum_ref[:, WIDE : 2 * WIDE]
    side = sum_ref[:, 2 * WIDE :]
    squares += side[:, GATE_ROWS : GATE_ROWS + 1]
    scale = lax.rsqrt(squares * (1.0 / HIDDEN) + EPS)
    tile = entered_ref[pl.ds(PIECE, FLAG_ROWS)]
    tile_ref[...] = tile
    keep = 1.0 - tile.astype(jnp.float32)[0:1, :HD]
    for h in range(HEADS):
        a = a_ref[h] * keep
        z = z_ref[h : h + 1] * keep
        k = keys[:, h * HD : (h + 1) * HD] * scale
        k = jnp.where(k > 0, k + 1.0, jnp.exp(jnp.minimum(k, 0.0)))
        top = jnp.dot(k, a, precision=HIGHEST, preferred_element_type=jnp.float32)
        bottom = jnp.sum(k * z, axis=1, keepdims=True) + 1.0
        read = top / bottom
        read_ref[:, h * HD : (h + 1) * HD] = read.astype(jnp.bfloat16)
        if write:
            v = values[rows - MEM :, h * HD : (h + 1) * HD] * scale[rows - MEM :]
            logit = (side[rows - MEM :, h : h + 1] + gates[:, h : h + 1]) * scale[rows - MEM :]
            gate = 1.0 / (1.0 + jnp.exp(-logit))
            tail = k[rows - MEM :]
            state[0][h] = a + lax.dot_general(
                tail,
                (v - read[rows - MEM :]) * gate,
                (((0,), (0,)), ((), ())),
                precision=HIGHEST,
                preferred_element_type=jnp.float32,
            )
            state[1][h : h + 1] = z + jnp.sum(tail, axis=0, keepdims=True)
    f_copy.wait()


def half_scratch(rows):
    weights = pltpu.VMEM((N_CHIPS, BLOCK, WIDE), jnp.bfloat16)
    x = pltpu.VMEM((N_CHIPS, rows, BLOCK), jnp.bfloat16)
    return [x, weights, weights, pltpu.SemaphoreType.DMA((3, N_CHIPS))]


def project_first(core, own, gain, wk, wv, gate, write):
    rows = own.shape[1]
    return pl.pallas_call(
        functools.partial(first_kernel, write),
        in_specs=[SMEM, ANY, VMEM, ANY, ANY, VMEM],
        out_specs=VMEM,
        out_shape=jax.ShapeDtypeStruct((rows, 2 * WIDE + SIDE), jnp.float32),
        scratch_shapes=half_scratch(rows),
        compiler_params=pltpu.CompilerParams(vmem_limit_bytes=VMEM_LIMIT),
        cost_estimate=pl.CostEstimate(
            flops=rows * HIDDEN * 2 * WIDE, bytes_accessed=6 * 2**20, transcendentals=0
        ),
    )(core, own, gain, wk, wv, gate)


def read_memory(core, entered, begun, got, gain, wk, wv, gate, f, a, z, write):
    rows = got.shape[1]
    shapes = [
        jax.ShapeDtypeStruct((rows, WIDE), jnp.bfloat16),
        jax.ShapeDtypeStruct(f.shape, f.dtype),
        jax.ShapeDtypeStruct((FLAG_ROWS, BLOCK), jnp.bfloat16),
    ]
    if write:
        shapes += [jax.ShapeDtypeStruct(a.shape, a.dtype), jax.ShapeDtypeStruct(z.shape, z.dtype)]
    return pl.pallas_call(
        functools.partial(read_kernel, write),
        in_specs=[SMEM, VMEM, VMEM, ANY, VMEM, ANY, ANY, VMEM, ANY, VMEM, VMEM],
        out_specs=[VMEM] * len(shapes),
        out_shape=shapes,
        scratch_shapes=half_scratch(rows) + [pltpu.SemaphoreType.DMA((1,))],
        compiler_params=pltpu.CompilerParams(vmem_limit_bytes=VMEM_LIMIT),
        cost_estimate=pl.CostEstimate(
            flops=rows * HIDDEN * 2 * WIDE, bytes_accessed=6 * 2**20, transcendentals=0
        ),
    )(core, entered, begun, got, gain, wk, wv, gate, f, a, z)


def output_kernel(near_ref, far_ref, keep_ref, got_ref, p_ref):
    near, far = near_ref[...], far_ref[...]
    for b in range(N_CHIPS):
        part = jnp.dot(near, keep_ref[b], preferred_element_type=jnp.float32)
        part += jnp.dot(far, got_ref[b], preferred_element_type=jnp.float32)
        p_ref[b] = part.astype(jnp.bfloat16)


def output(near, far, keep, got):
    rows = near.shape[0]
    return pl.pallas_call(
        output_kernel,
        in_specs=[VMEM] * 4,
        out_specs=VMEM,
        out_shape=jax.ShapeDtypeStruct((N_CHIPS, rows, BLOCK), jnp.bfloat16),
        compiler_params=pltpu.CompilerParams(vmem_limit_bytes=VMEM_LIMIT),
        cost_estimate=pl.CostEstimate(
            flops=2 * rows * 2 * WIDE * 4096, bytes_accessed=6 * 2**20, transcendentals=0
        ),
    )(near, far, keep, got)


def copies(x):
    return jnp.broadcast_to(x[None], (N_CHIPS,) + x.shape)


def exchange(blocks):
    return lax.all_to_all(blocks, CHIPS, 0, 0, tiled=True)


def local(
    initial_stack_inputs,
    initial_sequence_starts,
    arriving_pieces,
    recall_embeddings,
    rescaling_factors,
    lookup_projection,
    content_projection,
    write_gate_projection,
    final_projection,
    associative_stores,
    denominator_vectors,
):
    core = lax.axis_index("core")
    which = core.astype(jnp.int32).reshape(1)
    section_zero = (lax.axis_index("y_lo") == 0) & (lax.axis_index("z") == 0)
    steps = arriving_pieces.shape[0] // SEG + 1

    flag = (initial_sequence_starts[0] > 0).astype(jnp.bfloat16)
    tile = jnp.broadcast_to(flag, (FLAG_ROWS, BLOCK))
    entered = jnp.concatenate([initial_stack_inputs, tile], axis=0)
    outgoing, which = lax.optimization_barrier((copies(initial_stack_inputs), which))

    wk = lookup_projection[0].reshape(2 * N_CHIPS, BLOCK, WIDE)
    wv = content_projection[0].reshape(2 * N_CHIPS, BLOCK, WIDE)
    f_keep, f_sent = pick(which, final_projection[0])
    f_got = swap(f_sent, "core")
    gain = rescaling_factors.reshape(2 * N_CHIPS, 1, BLOCK)
    gate = write_gate_projection[0].T.reshape(HEADS, 2 * N_CHIPS, BLOCK).transpose(1, 0, 2)
    gate = jnp.pad(gate, ((0, 0), (0, GATE_ROWS - HEADS), (0, 0)))

    a = associative_stores[0]
    z = denominator_vectors[0]
    clear = jnp.zeros((FLAG_ROWS, BLOCK), jnp.bfloat16)
    entering = [
        jnp.concatenate(
            [arriving_pieces[t * SEG : (t + 1) * SEG], recall_embeddings, clear], axis=0
        )
        for t in range(steps - 1)
    ]
    for t in range(steps):
        write = t + 1 < steps
        if t > 0:
            moved = next_section(jnp.concatenate([x, tile], axis=0))
            entered = jnp.where(section_zero, entering[t - 1], moved)
            outgoing = copies(entered[:PIECE])
        own = exchange(outgoing)
        got = swap(own, "core")
        begun = project_first(which, own, gain, wk, wv, gate, write)
        read, f_near, tile, *state = read_memory(
            which, entered, begun, got, gain, wk, wv, gate, f_got, a, z, write
        )
        if write:
            a, z = state
        if t == 0:
            read, entering, section_zero = lax.optimization_barrier((read, entering, section_zero))
        p = exchange(output(read, swap(read, "core"), f_keep, f_near))
        total = jnp.sum(p.astype(jnp.float32), axis=0)
        x = (entered[:PIECE].astype(jnp.float32) + total).astype(jnp.bfloat16)
    return x


def solution(mesh):
    fine = Mesh(mesh.devices.reshape(2, 8, 4, 2, 2), AXES)
    return jax.shard_map(
        local,
        mesh=fine,
        in_specs=(
            P(SECTION, TENSOR),
            P(SECTION),
            P(None, TENSOR),
            P(None, TENSOR),
            P(SECTION, None),
            P(SECTION, None, TENSOR),
            P(SECTION, None, TENSOR),
            P(SECTION, None, TENSOR),
            P(SECTION, TENSOR, None),
            P(SECTION, TENSOR, None, None),
            P(SECTION, TENSOR, None),
        ),
        out_specs=P(SECTION, TENSOR),
        check_vma=False,
    )
```

```python
import functools

import jax
import jax.numpy as jnp
from jax import lax
from jax.experimental import pallas as pl
from jax.experimental.pallas import tpu as pltpu
from jax.sharding import Mesh
from jax.sharding import PartitionSpec as P

SEG = 128
PIECE = 192
MEM = 64
EPS = 1e-05
AXES = ("y_lo", "z", "x", "y_hi", "core")
SECTION = ("y_lo", "z")
TENSOR = ("x", "y_hi", "core")
CHIPS = ("x", "y_hi")
N_CHIPS = 8
FLAG_ROWS = 16
BLOCK = 512
HEADS = 2
SIDE = 128
GATE_ROWS = 16
HD = 128
WIDE = HEADS * HD
HIDDEN = 8192
VMEM_LIMIT = 48 * 2**20
HIGHEST = lax.Precision.HIGHEST


VMEM = pl.BlockSpec(memory_space=pltpu.VMEM)
SMEM = pl.BlockSpec(memory_space=pltpu.SMEM)


def swap(value, axis):
    return lax.ppermute(value, axis, [(0, 1), (1, 0)])


def next_section(value):
    return lax.ppermute(value, SECTION, [(i, i + 1) for i in range(15)])


ANY = pl.BlockSpec(memory_space=pl.ANY)


def pick_kernel(core_ref, f_ref, keep_ref, sent_ref):
    core = core_ref[0]
    keep_ref[0] = f_ref[:, pl.ds(pl.multiple_of(core * BLOCK, BLOCK), BLOCK)]
    sent_ref[0] = f_ref[:, pl.ds(pl.multiple_of((1 - core) * BLOCK, BLOCK), BLOCK)]


def pick(core, f):
    block = pl.BlockSpec((1, WIDE, BLOCK), lambda b: (b, 0, 0))
    shape = jax.ShapeDtypeStruct((N_CHIPS, WIDE, BLOCK), jnp.bfloat16)
    return pl.pallas_call(
        pick_kernel,
        grid=(N_CHIPS,),
        in_specs=[SMEM, pl.BlockSpec((WIDE, 2 * BLOCK), lambda b: (0, b))],
        out_specs=[block, block],
        out_shape=[shape, shape],
        compiler_params=pltpu.CompilerParams(vmem_limit_bytes=VMEM_LIMIT),
        cost_estimate=pl.CostEstimate(flops=0, bytes_accessed=0, transcendentals=0),
    )(core, f)


def project_half(write, offset, x_ref, gain_ref, wk_ref, wv_ref, gate_ref, bufs, sems, extra=None):
    k_buf, v_buf = bufs
    rows = x_ref.shape[1]
    copies = []
    for b in range(N_CHIPS):
        place = 2 * b + offset
        group = []
        for i, (source, target) in enumerate(
            (
                (wk_ref.at[place], k_buf.at[b]),
                (wv_ref.at[place], v_buf.at[b]),
            )
        ):
            copy = pltpu.make_async_copy(source, target, sems.at[i, b])
            copy.start()
            group.append(copy)
        copies.append(group)
    if extra is not None:
        extra.start()
    dot = functools.partial(jnp.dot, preferred_element_type=jnp.float32)
    squares, gates, keys, values = 0.0, 0.0, 0.0, 0.0
    for b in range(N_CHIPS):
        place = 2 * b + offset
        for copy in copies[b]:
            copy.wait()
        wide = x_ref[b].astype(jnp.float32)
        squares += wide * wide
        scaled = (wide * gain_ref[place]).astype(jnp.bfloat16)
        keys += dot(scaled, k_buf[b])
        values += dot(scaled, v_buf[b])
        if write:
            gates += lax.dot_general(
                scaled[rows - MEM :],
                gate_ref[place],
                (((1,), (1,)), ((), ())),
                preferred_element_type=jnp.float32,
            )
    return keys, values, jnp.sum(squares, axis=1, keepdims=True), gates


def first_kernel(write, core_ref, x_ref, gain_ref, wk_ref, wv_ref, gate_ref, sum_ref, *rest):
    *bufs, sems = rest
    rows = x_ref.shape[1]
    keys, values, squares, gates = project_half(
        write, core_ref[0], x_ref, gain_ref, wk_ref, wv_ref, gate_ref, bufs, sems
    )
    sum_ref[:, :WIDE] = keys
    sum_ref[:, WIDE : 2 * WIDE] = values
    lane = lax.broadcasted_iota(jnp.int32, (rows, SIDE), 1)
    side = jnp.where(lane == GATE_ROWS, squares, 0.0)
    sum_ref[:, 2 * WIDE :] = side
    if write:
        sum_ref[rows - MEM :, 2 * WIDE : 2 * WIDE + GATE_ROWS] = gates


def read_kernel(
    write, core_ref, entered_ref, sum_ref, x_ref, gain_ref, wk_ref, wv_ref, gate_ref, f_ref,
    a_ref, z_ref, read_ref, f_next, tile_ref, *rest,
):
    *state, k_buf, v_buf, sems, f_sem = rest
    rows = x_ref.shape[1]
    f_copy = pltpu.make_async_copy(f_ref, f_next, f_sem.at[0])
    keys, values, squares, gates = project_half(
        write, 1 - core_ref[0], x_ref, gain_ref, wk_ref, wv_ref, gate_ref,
        (k_buf, v_buf), sems, f_copy,
    )
    keys += sum_ref[:, :WIDE]
    values += sum_ref[:, WIDE : 2 * WIDE]
    side = sum_ref[:, 2 * WIDE :]
    squares += side[:, GATE_ROWS : GATE_ROWS + 1]
    scale = lax.rsqrt(squares * (1.0 / HIDDEN) + EPS)
    tile = entered_ref[pl.ds(PIECE, FLAG_ROWS)]
    tile_ref[...] = tile
    keep = 1.0 - tile.astype(jnp.float32)[0:1, :HD]
    for h in range(HEADS):
        a = a_ref[h] * keep
        z = z_ref[h : h + 1] * keep
        k = keys[:, h * HD : (h + 1) * HD] * scale
        k = jnp.where(k > 0, k + 1.0, jnp.exp(jnp.minimum(k, 0.0)))
        top = jnp.dot(k, a, precision=HIGHEST, preferred_element_type=jnp.float32)
        bottom = jnp.sum(k * z, axis=1, keepdims=True) + 1.0
        read = top / bottom
        read_ref[:, h * HD : (h + 1) * HD] = read.astype(jnp.bfloat16)
        if write:
            v = values[rows - MEM :, h * HD : (h + 1) * HD] * scale[rows - MEM :]
            logit = (side[rows - MEM :, h : h + 1] + gates[:, h : h + 1]) * scale[rows - MEM :]
            gate = 1.0 / (1.0 + jnp.exp(-logit))
            tail = k[rows - MEM :]
            state[0][h] = a + lax.dot_general(
                tail,
                (v - read[rows - MEM :]) * gate,
                (((0,), (0,)), ((), ())),
                precision=HIGHEST,
                preferred_element_type=jnp.float32,
            )
            state[1][h : h + 1] = z + jnp.sum(tail, axis=0, keepdims=True)
    f_copy.wait()


def half_scratch():
    weights = pltpu.VMEM((N_CHIPS, BLOCK, WIDE), jnp.bfloat16)
    return [weights, weights, pltpu.SemaphoreType.DMA((2, N_CHIPS))]


def project_first(core, own, gain, wk, wv, gate, write):
    rows = own.shape[1]
    return pl.pallas_call(
        functools.partial(first_kernel, write),
        in_specs=[SMEM, VMEM, VMEM, ANY, ANY, VMEM],
        out_specs=VMEM,
        out_shape=jax.ShapeDtypeStruct((rows, 2 * WIDE + SIDE), jnp.float32),
        scratch_shapes=half_scratch(),
        compiler_params=pltpu.CompilerParams(vmem_limit_bytes=VMEM_LIMIT),
        cost_estimate=pl.CostEstimate(
            flops=rows * HIDDEN * 2 * WIDE, bytes_accessed=6 * 2**20, transcendentals=0
        ),
    )(core, own, gain, wk, wv, gate)


def read_memory(core, entered, begun, got, gain, wk, wv, gate, f, a, z, write):
    rows = got.shape[1]
    shapes = [
        jax.ShapeDtypeStruct((rows, WIDE), jnp.bfloat16),
        jax.ShapeDtypeStruct(f.shape, f.dtype),
        jax.ShapeDtypeStruct((FLAG_ROWS, BLOCK), jnp.bfloat16),
    ]
    if write:
        shapes += [jax.ShapeDtypeStruct(a.shape, a.dtype), jax.ShapeDtypeStruct(z.shape, z.dtype)]
    return pl.pallas_call(
        functools.partial(read_kernel, write),
        in_specs=[SMEM, VMEM, VMEM, VMEM, VMEM, ANY, ANY, VMEM, ANY, VMEM, VMEM],
        out_specs=[VMEM] * len(shapes),
        out_shape=shapes,
        scratch_shapes=half_scratch() + [pltpu.SemaphoreType.DMA((1,))],
        compiler_params=pltpu.CompilerParams(vmem_limit_bytes=VMEM_LIMIT),
        cost_estimate=pl.CostEstimate(
            flops=rows * HIDDEN * 2 * WIDE, bytes_accessed=6 * 2**20, transcendentals=0
        ),
    )(core, entered, begun, got, gain, wk, wv, gate, f, a, z)


def output_kernel(near_ref, far_ref, keep_ref, got_ref, p_ref):
    near, far = near_ref[...], far_ref[...]
    for b in range(N_CHIPS):
        part = jnp.dot(near, keep_ref[b], preferred_element_type=jnp.float32)
        part += jnp.dot(far, got_ref[b], preferred_element_type=jnp.float32)
        p_ref[b] = part.astype(jnp.bfloat16)


def output(near, far, keep, got):
    rows = near.shape[0]
    return pl.pallas_call(
        output_kernel,
        in_specs=[VMEM] * 4,
        out_specs=VMEM,
        out_shape=jax.ShapeDtypeStruct((N_CHIPS, rows, BLOCK), jnp.bfloat16),
        compiler_params=pltpu.CompilerParams(vmem_limit_bytes=VMEM_LIMIT),
        cost_estimate=pl.CostEstimate(
            flops=2 * rows * 2 * WIDE * 4096, bytes_accessed=6 * 2**20, transcendentals=0
        ),
    )(near, far, keep, got)


def copies(x):
    return jnp.broadcast_to(x[None], (N_CHIPS,) + x.shape)


def exchange(blocks):
    return lax.all_to_all(blocks, CHIPS, 0, 0, tiled=True)


def local(
    initial_stack_inputs,
    initial_sequence_starts,
    arriving_pieces,
    recall_embeddings,
    rescaling_factors,
    lookup_projection,
    content_projection,
    write_gate_projection,
    final_projection,
    associative_stores,
    denominator_vectors,
):
    core = lax.axis_index("core")
    which = core.astype(jnp.int32).reshape(1)
    section_zero = (lax.axis_index("y_lo") == 0) & (lax.axis_index("z") == 0)
    steps = arriving_pieces.shape[0] // SEG + 1

    flag = (initial_sequence_starts[0] > 0).astype(jnp.bfloat16)
    tile = jnp.broadcast_to(flag, (FLAG_ROWS, BLOCK))
    entered = jnp.concatenate([initial_stack_inputs, tile], axis=0)
    outgoing, which = lax.optimization_barrier((copies(initial_stack_inputs), which))

    wk = lookup_projection[0].reshape(2 * N_CHIPS, BLOCK, WIDE)
    wv = content_projection[0].reshape(2 * N_CHIPS, BLOCK, WIDE)
    f_keep, f_sent = pick(which, final_projection[0])
    f_got = swap(f_sent, "core")
    gain = rescaling_factors.reshape(2 * N_CHIPS, 1, BLOCK)
    gate = write_gate_projection[0].T.reshape(HEADS, 2 * N_CHIPS, BLOCK).transpose(1, 0, 2)
    gate = jnp.pad(gate, ((0, 0), (0, GATE_ROWS - HEADS), (0, 0)))

    a = associative_stores[0]
    z = denominator_vectors[0]
    clear = jnp.zeros((FLAG_ROWS, BLOCK), jnp.bfloat16)
    entering = [
        jnp.concatenate(
            [arriving_pieces[t * SEG : (t + 1) * SEG], recall_embeddings, clear], axis=0
        )
        for t in range(steps - 1)
    ]
    for t in range(steps):
        write = t + 1 < steps
        if t > 0:
            moved = next_section(jnp.concatenate([x, tile], axis=0))
            entered = jnp.where(section_zero, entering[t - 1], moved)
            outgoing = copies(entered[:PIECE])
        own = exchange(outgoing)
        got = swap(own, "core")
        begun = project_first(which, own, gain, wk, wv, gate, write)
        read, f_near, tile, *state = read_memory(
            which, entered, begun, got, gain, wk, wv, gate, f_got, a, z, write
        )
        if write:
            a, z = state
        if t == 0:
            read, entering, section_zero = lax.optimization_barrier((read, entering, section_zero))
        p = exchange(output(read, swap(read, "core"), f_keep, f_near))
        total = jnp.sum(p.astype(jnp.float32), axis=0)
        x = (entered[:PIECE].astype(jnp.float32) + total).astype(jnp.bfloat16)
    return x


def solution(mesh):
    fine = Mesh(mesh.devices.reshape(2, 8, 4, 2, 2), AXES)
    return jax.shard_map(
        local,
        mesh=fine,
        in_specs=(
            P(SECTION, TENSOR),
            P(SECTION),
            P(None, TENSOR),
            P(None, TENSOR),
            P(SECTION, None),
            P(SECTION, None, TENSOR),
            P(SECTION, None, TENSOR),
            P(SECTION, None, TENSOR),
            P(SECTION, TENSOR, None),
            P(SECTION, TENSOR, None, None),
            P(SECTION, TENSOR, None),
        ),
        out_specs=P(SECTION, TENSOR),
        check_vma=False,
    )
```

```python
import functools

import jax
import jax.numpy as jnp
from jax import lax
from jax.experimental import pallas as pl
from jax.experimental.pallas import tpu as pltpu
from jax.sharding import Mesh
from jax.sharding import PartitionSpec as P

SEG = 128
PIECE = 192
MEM = 64
EPS = 1e-05
AXES = ("y_lo", "z", "x", "y_hi", "core")
SECTION = ("y_lo", "z")
TENSOR = ("x", "y_hi", "core")
CHIPS = ("x", "y_hi")
N_CHIPS = 8
FLAG_ROWS = 16
BLOCK = 512
HEADS = 2
SIDE = 128
GATE_ROWS = 16
HD = 128
WIDE = HEADS * HD
HIDDEN = 8192
VMEM_LIMIT = 48 * 2**20
HIGHEST = lax.Precision.HIGHEST


VMEM = pl.BlockSpec(memory_space=pltpu.VMEM)
SMEM = pl.BlockSpec(memory_space=pltpu.SMEM)


def swap(value, axis):
    return lax.ppermute(value, axis, [(0, 1), (1, 0)])


def next_section(value):
    return lax.ppermute(value, SECTION, [(i, i + 1) for i in range(15)])


ANY = pl.BlockSpec(memory_space=pl.ANY)


def pick_kernel(core_ref, f_ref, keep_ref, sent_ref):
    core = core_ref[0]
    keep_ref[0] = f_ref[:, pl.ds(pl.multiple_of(core * BLOCK, BLOCK), BLOCK)]
    sent_ref[0] = f_ref[:, pl.ds(pl.multiple_of((1 - core) * BLOCK, BLOCK), BLOCK)]


def pick(core, f):
    block = pl.BlockSpec((1, WIDE, BLOCK), lambda b: (b, 0, 0))
    shape = jax.ShapeDtypeStruct((N_CHIPS, WIDE, BLOCK), jnp.bfloat16)
    return pl.pallas_call(
        pick_kernel,
        grid=(N_CHIPS,),
        in_specs=[SMEM, pl.BlockSpec((WIDE, 2 * BLOCK), lambda b: (0, b))],
        out_specs=[block, block],
        out_shape=[shape, shape],
        compiler_params=pltpu.CompilerParams(vmem_limit_bytes=VMEM_LIMIT),
        cost_estimate=pl.CostEstimate(flops=0, bytes_accessed=0, transcendentals=0),
    )(core, f)


def project_half(write, offset, x_ref, gain_ref, wk_ref, wv_ref, gate_ref, bufs, sems, extra=None):
    k_buf, v_buf, *x_buf = bufs
    rows = x_ref.shape[1]
    copies = []
    for b in range(N_CHIPS):
        place = 2 * b + offset
        group = []
        for i, (source, target) in enumerate(
            (
                (wk_ref.at[place], k_buf.at[b]),
                (wv_ref.at[place], v_buf.at[b]),
                *((x_ref.at[b], buf.at[b]) for buf in x_buf),
            )
        ):
            copy = pltpu.make_async_copy(source, target, sems.at[i, b])
            copy.start()
            group.append(copy)
        copies.append(group)
    if extra is not None:
        extra.start()
    x_blocks = x_buf[0] if x_buf else x_ref
    dot = functools.partial(jnp.dot, preferred_element_type=jnp.float32)
    squares, gates, keys, values = 0.0, 0.0, 0.0, 0.0
    for b in range(N_CHIPS):
        place = 2 * b + offset
        for copy in copies[b]:
            copy.wait()
        wide = x_blocks[b].astype(jnp.float32)
        squares += wide * wide
        scaled = (wide * gain_ref[place]).astype(jnp.bfloat16)
        keys += dot(scaled, k_buf[b])
        values += dot(scaled, v_buf[b])
        if write:
            gates += lax.dot_general(
                scaled[rows - MEM :],
                gate_ref[place],
                (((1,), (1,)), ((), ())),
                preferred_element_type=jnp.float32,
            )
    return keys, values, jnp.sum(squares, axis=1, keepdims=True), gates


def first_kernel(write, core_ref, x_ref, gain_ref, wk_ref, wv_ref, gate_ref, sum_ref, *rest):
    *bufs, sems = rest
    rows = x_ref.shape[1]
    keys, values, squares, gates = project_half(
        write, core_ref[0], x_ref, gain_ref, wk_ref, wv_ref, gate_ref, bufs, sems
    )
    sum_ref[:, :WIDE] = keys
    sum_ref[:, WIDE : 2 * WIDE] = values
    lane = lax.broadcasted_iota(jnp.int32, (rows, SIDE), 1)
    side = jnp.where(lane == GATE_ROWS, squares, 0.0)
    sum_ref[:, 2 * WIDE :] = side
    if write:
        sum_ref[rows - MEM :, 2 * WIDE : 2 * WIDE + GATE_ROWS] = gates


def read_kernel(
    write, buffers, core_ref, entered_ref, sum_ref, x_ref, gain_ref, wk_ref, wv_ref, gate_ref, f_ref,
    a_ref, z_ref, read_ref, f_next, tile_ref, *rest,
):
    *state, sems, f_sem = rest
    state, bufs = state[:-buffers], state[-buffers:]
    rows = x_ref.shape[1]
    f_copy = pltpu.make_async_copy(f_ref, f_next, f_sem.at[0])
    keys, values, squares, gates = project_half(
        write, 1 - core_ref[0], x_ref, gain_ref, wk_ref, wv_ref, gate_ref,
        bufs, sems, f_copy,
    )
    keys += sum_ref[:, :WIDE]
    values += sum_ref[:, WIDE : 2 * WIDE]
    side = sum_ref[:, 2 * WIDE :]
    squares += side[:, GATE_ROWS : GATE_ROWS + 1]
    scale = lax.rsqrt(squares * (1.0 / HIDDEN) + EPS)
    tile = entered_ref[pl.ds(PIECE, FLAG_ROWS)]
    tile_ref[...] = tile
    keep = 1.0 - tile.astype(jnp.float32)[0:1, :HD]
    for h in range(HEADS):
        a = a_ref[h] * keep
        z = z_ref[h : h + 1] * keep
        k = keys[:, h * HD : (h + 1) * HD] * scale
        k = jnp.where(k > 0, k + 1.0, jnp.exp(jnp.minimum(k, 0.0)))
        top = jnp.dot(k, a, precision=HIGHEST, preferred_element_type=jnp.float32)
        bottom = jnp.sum(k * z, axis=1, keepdims=True) + 1.0
        read = top / bottom
        read_ref[:, h * HD : (h + 1) * HD] = read.astype(jnp.bfloat16)
        if write:
            v = values[rows - MEM :, h * HD : (h + 1) * HD] * scale[rows - MEM :]
            logit = (side[rows - MEM :, h : h + 1] + gates[:, h : h + 1]) * scale[rows - MEM :]
            gate = 1.0 / (1.0 + jnp.exp(-logit))
            tail = k[rows - MEM :]
            state[0][h] = a + lax.dot_general(
                tail,
                (v - read[rows - MEM :]) * gate,
                (((0,), (0,)), ((), ())),
                precision=HIGHEST,
                preferred_element_type=jnp.float32,
            )
            state[1][h : h + 1] = z + jnp.sum(tail, axis=0, keepdims=True)
    f_copy.wait()


def half_scratch(rows, stream):
    weights = pltpu.VMEM((N_CHIPS, BLOCK, WIDE), jnp.bfloat16)
    x = [pltpu.VMEM((N_CHIPS, rows, BLOCK), jnp.bfloat16)] if stream else []
    return [weights, weights, *x, pltpu.SemaphoreType.DMA((3, N_CHIPS))]


def project_first(core, own, gain, wk, wv, gate, write, stream):
    rows = own.shape[1]
    return pl.pallas_call(
        functools.partial(first_kernel, write),
        in_specs=[SMEM, ANY if stream else VMEM, VMEM, ANY, ANY, VMEM],
        out_specs=VMEM,
        out_shape=jax.ShapeDtypeStruct((rows, 2 * WIDE + SIDE), jnp.float32),
        scratch_shapes=half_scratch(rows, stream),
        compiler_params=pltpu.CompilerParams(vmem_limit_bytes=VMEM_LIMIT),
        cost_estimate=pl.CostEstimate(
            flops=rows * HIDDEN * 2 * WIDE, bytes_accessed=6 * 2**20, transcendentals=0
        ),
    )(core, own, gain, wk, wv, gate)


def read_memory(core, entered, begun, got, gain, wk, wv, gate, f, a, z, write, stream):
    rows = got.shape[1]
    shapes = [
        jax.ShapeDtypeStruct((rows, WIDE), jnp.bfloat16),
        jax.ShapeDtypeStruct(f.shape, f.dtype),
        jax.ShapeDtypeStruct((FLAG_ROWS, BLOCK), jnp.bfloat16),
    ]
    if write:
        shapes += [jax.ShapeDtypeStruct(a.shape, a.dtype), jax.ShapeDtypeStruct(z.shape, z.dtype)]
    return pl.pallas_call(
        functools.partial(read_kernel, write, 3 if stream else 2),
        in_specs=[SMEM, VMEM, VMEM, ANY if stream else VMEM, VMEM, ANY, ANY, VMEM, ANY, VMEM, VMEM],
        out_specs=[VMEM] * len(shapes),
        out_shape=shapes,
        scratch_shapes=half_scratch(rows, stream) + [pltpu.SemaphoreType.DMA((1,))],
        compiler_params=pltpu.CompilerParams(vmem_limit_bytes=VMEM_LIMIT),
        cost_estimate=pl.CostEstimate(
            flops=rows * HIDDEN * 2 * WIDE, bytes_accessed=6 * 2**20, transcendentals=0
        ),
    )(core, entered, begun, got, gain, wk, wv, gate, f, a, z)


def output_kernel(near_ref, far_ref, keep_ref, got_ref, p_ref):
    near, far = near_ref[...], far_ref[...]
    for b in range(N_CHIPS):
        part = jnp.dot(near, keep_ref[b], preferred_element_type=jnp.float32)
        part += jnp.dot(far, got_ref[b], preferred_element_type=jnp.float32)
        p_ref[b] = part.astype(jnp.bfloat16)


def output(near, far, keep, got):
    rows = near.shape[0]
    return pl.pallas_call(
        output_kernel,
        in_specs=[VMEM] * 4,
        out_specs=VMEM,
        out_shape=jax.ShapeDtypeStruct((N_CHIPS, rows, BLOCK), jnp.bfloat16),
        compiler_params=pltpu.CompilerParams(vmem_limit_bytes=VMEM_LIMIT),
        cost_estimate=pl.CostEstimate(
            flops=2 * rows * 2 * WIDE * 4096, bytes_accessed=6 * 2**20, transcendentals=0
        ),
    )(near, far, keep, got)


def copies(x):
    return jnp.broadcast_to(x[None], (N_CHIPS,) + x.shape)


def exchange(blocks):
    return lax.all_to_all(blocks, CHIPS, 0, 0, tiled=True)


def local(
    initial_stack_inputs,
    initial_sequence_starts,
    arriving_pieces,
    recall_embeddings,
    rescaling_factors,
    lookup_projection,
    content_projection,
    write_gate_projection,
    final_projection,
    associative_stores,
    denominator_vectors,
):
    core = lax.axis_index("core")
    which = core.astype(jnp.int32).reshape(1)
    section_zero = (lax.axis_index("y_lo") == 0) & (lax.axis_index("z") == 0)
    steps = arriving_pieces.shape[0] // SEG + 1

    flag = (initial_sequence_starts[0] > 0).astype(jnp.bfloat16)
    tile = jnp.broadcast_to(flag, (FLAG_ROWS, BLOCK))
    entered = jnp.concatenate([initial_stack_inputs, tile], axis=0)
    outgoing, which = lax.optimization_barrier((copies(initial_stack_inputs), which))

    wk = lookup_projection[0].reshape(2 * N_CHIPS, BLOCK, WIDE)
    wv = content_projection[0].reshape(2 * N_CHIPS, BLOCK, WIDE)
    f_keep, f_sent = pick(which, final_projection[0])
    f_got = swap(f_sent, "core")
    gain = rescaling_factors.reshape(2 * N_CHIPS, 1, BLOCK)
    gate = write_gate_projection[0].T.reshape(HEADS, 2 * N_CHIPS, BLOCK).transpose(1, 0, 2)
    gate = jnp.pad(gate, ((0, 0), (0, GATE_ROWS - HEADS), (0, 0)))

    a = associative_stores[0]
    z = denominator_vectors[0]
    clear = jnp.zeros((FLAG_ROWS, BLOCK), jnp.bfloat16)
    entering = [
        jnp.concatenate(
            [arriving_pieces[t * SEG : (t + 1) * SEG], recall_embeddings, clear], axis=0
        )
        for t in range(steps - 1)
    ]
    for t in range(steps):
        write = t + 1 < steps
        if t > 0:
            moved = next_section(jnp.concatenate([x, tile], axis=0))
            entered = jnp.where(section_zero, entering[t - 1], moved)
            outgoing = copies(entered[:PIECE])
        own = exchange(outgoing)
        got = swap(own, "core")
        begun = project_first(which, own, gain, wk, wv, gate, write, t == 0)
        read, f_near, tile, *state = read_memory(
            which, entered, begun, got, gain, wk, wv, gate, f_got, a, z, write, t == 0
        )
        if write:
            a, z = state
        if t == 0:
            read, entering, section_zero = lax.optimization_barrier((read, entering, section_zero))
        p = exchange(output(read, swap(read, "core"), f_keep, f_near))
        total = jnp.sum(p.astype(jnp.float32), axis=0)
        x = (entered[:PIECE].astype(jnp.float32) + total).astype(jnp.bfloat16)
    return x


def solution(mesh):
    fine = Mesh(mesh.devices.reshape(2, 8, 4, 2, 2), AXES)
    return jax.shard_map(
        local,
        mesh=fine,
        in_specs=(
            P(SECTION, TENSOR),
            P(SECTION),
            P(None, TENSOR),
            P(None, TENSOR),
            P(SECTION, None),
            P(SECTION, None, TENSOR),
            P(SECTION, None, TENSOR),
            P(SECTION, None, TENSOR),
            P(SECTION, TENSOR, None),
            P(SECTION, TENSOR, None, None),
            P(SECTION, TENSOR, None),
        ),
        out_specs=P(SECTION, TENSOR),
        check_vma=False,
    )
```

```python
import functools

import jax
import jax.numpy as jnp
from jax import lax
from jax.experimental import pallas as pl
from jax.experimental.pallas import tpu as pltpu
from jax.sharding import Mesh
from jax.sharding import PartitionSpec as P

SEG = 128
PIECE = 192
MEM = 64
EPS = 1e-05
AXES = ("y_lo", "z", "x", "y_hi", "core")
SECTION = ("y_lo", "z")
TENSOR = ("x", "y_hi", "core")
CHIPS = ("x", "y_hi")
N_CHIPS = 8
FLAG_ROWS = 16
BLOCK = 512
HEADS = 2
SIDE = 128
GATE_ROWS = 16
HD = 128
WIDE = HEADS * HD
HIDDEN = 8192
VMEM_LIMIT = 48 * 2**20


VMEM = pl.BlockSpec(memory_space=pltpu.VMEM)
SMEM = pl.BlockSpec(memory_space=pltpu.SMEM)


def swap(value, axis):
    return lax.ppermute(value, axis, [(0, 1), (1, 0)])


def next_section(value):
    return lax.ppermute(value, SECTION, [(i, i + 1) for i in range(15)])


ANY = pl.BlockSpec(memory_space=pl.ANY)


def pick_kernel(core_ref, f_ref, keep_ref, sent_ref):
    core = core_ref[0]
    keep_ref[0] = f_ref[:, pl.ds(pl.multiple_of(core * BLOCK, BLOCK), BLOCK)]
    sent_ref[0] = f_ref[:, pl.ds(pl.multiple_of((1 - core) * BLOCK, BLOCK), BLOCK)]


def pick(core, f):
    block = pl.BlockSpec((1, WIDE, BLOCK), lambda b: (b, 0, 0))
    shape = jax.ShapeDtypeStruct((N_CHIPS, WIDE, BLOCK), jnp.bfloat16)
    return pl.pallas_call(
        pick_kernel,
        grid=(N_CHIPS,),
        in_specs=[SMEM, pl.BlockSpec((WIDE, 2 * BLOCK), lambda b: (0, b))],
        out_specs=[block, block],
        out_shape=[shape, shape],
        compiler_params=pltpu.CompilerParams(vmem_limit_bytes=VMEM_LIMIT),
        cost_estimate=pl.CostEstimate(flops=0, bytes_accessed=0, transcendentals=0),
    )(core, f)


def project_half(write, offset, x_ref, gain_ref, wk_ref, wv_ref, gate_ref, bufs, sems, extra=None):
    k_buf, v_buf, *x_buf = bufs
    rows = x_ref.shape[1]
    copies = []
    for b in range(N_CHIPS):
        place = 2 * b + offset
        group = []
        for i, (source, target) in enumerate(
            (
                (wk_ref.at[place], k_buf.at[b]),
                (wv_ref.at[place], v_buf.at[b]),
                *((x_ref.at[b], buf.at[b]) for buf in x_buf),
            )
        ):
            copy = pltpu.make_async_copy(source, target, sems.at[i, b])
            copy.start()
            group.append(copy)
        copies.append(group)
    if extra is not None:
        extra.start()
    x_blocks = x_buf[0] if x_buf else x_ref
    dot = functools.partial(jnp.dot, preferred_element_type=jnp.float32)
    squares, gates, keys, values = 0.0, 0.0, 0.0, 0.0
    for b in range(N_CHIPS):
        place = 2 * b + offset
        for copy in copies[b]:
            copy.wait()
        wide = x_blocks[b].astype(jnp.float32)
        squares += wide * wide
        scaled = (wide * gain_ref[place]).astype(jnp.bfloat16)
        keys += dot(scaled, k_buf[b])
        values += dot(scaled, v_buf[b])
        if write:
            gates += lax.dot_general(
                scaled[rows - MEM :],
                gate_ref[place],
                (((1,), (1,)), ((), ())),
                preferred_element_type=jnp.float32,
            )
    return keys, values, jnp.sum(squares, axis=1, keepdims=True), gates


def first_kernel(write, core_ref, x_ref, gain_ref, wk_ref, wv_ref, gate_ref, sum_ref, *rest):
    *bufs, sems = rest
    rows = x_ref.shape[1]
    keys, values, squares, gates = project_half(
        write, core_ref[0], x_ref, gain_ref, wk_ref, wv_ref, gate_ref, bufs, sems
    )
    sum_ref[:, :WIDE] = keys
    sum_ref[:, WIDE : 2 * WIDE] = values
    lane = lax.broadcasted_iota(jnp.int32, (rows, SIDE), 1)
    side = jnp.where(lane == GATE_ROWS, squares, 0.0)
    sum_ref[:, 2 * WIDE :] = side
    if write:
        sum_ref[rows - MEM :, 2 * WIDE : 2 * WIDE + GATE_ROWS] = gates


def split_dot(left, right, contract):
    dot = functools.partial(
        lax.dot_general,
        dimension_numbers=((contract, (0,)), ((), ())),
        preferred_element_type=jnp.float32,
    )
    left_high, right_high = left.astype(jnp.bfloat16), right.astype(jnp.bfloat16)
    left_low = (left - left_high.astype(jnp.float32)).astype(jnp.bfloat16)
    right_low = (right - right_high.astype(jnp.float32)).astype(jnp.bfloat16)
    return dot(left_high, right_high) + (dot(left_high, right_low) + dot(left_low, right_high))


def read_kernel(
    write, buffers, core_ref, entered_ref, sum_ref, x_ref, gain_ref, wk_ref, wv_ref, gate_ref, f_ref,
    a_ref, z_ref, read_ref, f_next, tile_ref, *rest,
):
    *state, sems, f_sem = rest
    state, bufs = state[:-buffers], state[-buffers:]
    rows = x_ref.shape[1]
    f_copy = pltpu.make_async_copy(f_ref, f_next, f_sem.at[0])
    keys, values, squares, gates = project_half(
        write, 1 - core_ref[0], x_ref, gain_ref, wk_ref, wv_ref, gate_ref,
        bufs, sems, f_copy,
    )
    keys += sum_ref[:, :WIDE]
    values += sum_ref[:, WIDE : 2 * WIDE]
    side = sum_ref[:, 2 * WIDE :]
    squares += side[:, GATE_ROWS : GATE_ROWS + 1]
    scale = lax.rsqrt(squares * (1.0 / HIDDEN) + EPS)
    tile = entered_ref[pl.ds(PIECE, FLAG_ROWS)]
    tile_ref[...] = tile
    keep = 1.0 - tile.astype(jnp.float32)[0:1, :HD]
    for h in range(HEADS):
        a = a_ref[h] * keep
        z = z_ref[h : h + 1] * keep
        k = keys[:, h * HD : (h + 1) * HD] * scale
        k = jnp.where(k > 0, k + 1.0, jnp.exp(jnp.minimum(k, 0.0)))
        top = split_dot(k, a, (1,))
        bottom = jnp.sum(k * z, axis=1, keepdims=True) + 1.0
        read = top / bottom
        read_ref[:, h * HD : (h + 1) * HD] = read.astype(jnp.bfloat16)
        if write:
            v = values[rows - MEM :, h * HD : (h + 1) * HD] * scale[rows - MEM :]
            logit = (side[rows - MEM :, h : h + 1] + gates[:, h : h + 1]) * scale[rows - MEM :]
            gate = 1.0 / (1.0 + jnp.exp(-logit))
            tail = k[rows - MEM :]
            state[0][h] = a + split_dot(tail, (v - read[rows - MEM :]) * gate, (0,))
            state[1][h : h + 1] = z + jnp.sum(tail, axis=0, keepdims=True)
    f_copy.wait()


def half_scratch(rows, stream):
    weights = pltpu.VMEM((N_CHIPS, BLOCK, WIDE), jnp.bfloat16)
    x = [pltpu.VMEM((N_CHIPS, rows, BLOCK), jnp.bfloat16)] if stream else []
    return [weights, weights, *x, pltpu.SemaphoreType.DMA((3, N_CHIPS))]


def project_first(core, own, gain, wk, wv, gate, write, stream):
    rows = own.shape[1]
    return pl.pallas_call(
        functools.partial(first_kernel, write),
        in_specs=[SMEM, ANY if stream else VMEM, VMEM, ANY, ANY, VMEM],
        out_specs=VMEM,
        out_shape=jax.ShapeDtypeStruct((rows, 2 * WIDE + SIDE), jnp.float32),
        scratch_shapes=half_scratch(rows, stream),
        compiler_params=pltpu.CompilerParams(vmem_limit_bytes=VMEM_LIMIT),
        cost_estimate=pl.CostEstimate(
            flops=rows * HIDDEN * 2 * WIDE, bytes_accessed=6 * 2**20, transcendentals=0
        ),
    )(core, own, gain, wk, wv, gate)


def read_memory(core, entered, begun, got, gain, wk, wv, gate, f, a, z, write, stream):
    rows = got.shape[1]
    shapes = [
        jax.ShapeDtypeStruct((rows, WIDE), jnp.bfloat16),
        jax.ShapeDtypeStruct(f.shape, f.dtype),
        jax.ShapeDtypeStruct((FLAG_ROWS, BLOCK), jnp.bfloat16),
    ]
    if write:
        shapes += [jax.ShapeDtypeStruct(a.shape, a.dtype), jax.ShapeDtypeStruct(z.shape, z.dtype)]
    return pl.pallas_call(
        functools.partial(read_kernel, write, 3 if stream else 2),
        in_specs=[SMEM, VMEM, VMEM, ANY if stream else VMEM, VMEM, ANY, ANY, VMEM, ANY, VMEM, VMEM],
        out_specs=[VMEM] * len(shapes),
        out_shape=shapes,
        scratch_shapes=half_scratch(rows, stream) + [pltpu.SemaphoreType.DMA((1,))],
        compiler_params=pltpu.CompilerParams(vmem_limit_bytes=VMEM_LIMIT),
        cost_estimate=pl.CostEstimate(
            flops=rows * HIDDEN * 2 * WIDE, bytes_accessed=6 * 2**20, transcendentals=0
        ),
    )(core, entered, begun, got, gain, wk, wv, gate, f, a, z)


def output_kernel(near_ref, far_ref, keep_ref, got_ref, p_ref):
    near, far = near_ref[...], far_ref[...]
    for b in range(N_CHIPS):
        part = jnp.dot(near, keep_ref[b], preferred_element_type=jnp.float32)
        part += jnp.dot(far, got_ref[b], preferred_element_type=jnp.float32)
        p_ref[b] = part.astype(jnp.bfloat16)


def output(near, far, keep, got):
    rows = near.shape[0]
    return pl.pallas_call(
        output_kernel,
        in_specs=[VMEM] * 4,
        out_specs=VMEM,
        out_shape=jax.ShapeDtypeStruct((N_CHIPS, rows, BLOCK), jnp.bfloat16),
        compiler_params=pltpu.CompilerParams(vmem_limit_bytes=VMEM_LIMIT),
        cost_estimate=pl.CostEstimate(
            flops=2 * rows * 2 * WIDE * 4096, bytes_accessed=6 * 2**20, transcendentals=0
        ),
    )(near, far, keep, got)


def copies(x):
    return jnp.broadcast_to(x[None], (N_CHIPS,) + x.shape)


def exchange(blocks):
    return lax.all_to_all(blocks, CHIPS, 0, 0, tiled=True)


def local(
    initial_stack_inputs,
    initial_sequence_starts,
    arriving_pieces,
    recall_embeddings,
    rescaling_factors,
    lookup_projection,
    content_projection,
    write_gate_projection,
    final_projection,
    associative_stores,
    denominator_vectors,
):
    core = lax.axis_index("core")
    which = core.astype(jnp.int32).reshape(1)
    section_zero = (lax.axis_index("y_lo") == 0) & (lax.axis_index("z") == 0)
    steps = arriving_pieces.shape[0] // SEG + 1

    flag = (initial_sequence_starts[0] > 0).astype(jnp.bfloat16)
    tile = jnp.broadcast_to(flag, (FLAG_ROWS, BLOCK))
    entered = jnp.concatenate([initial_stack_inputs, tile], axis=0)
    outgoing, which = lax.optimization_barrier((copies(initial_stack_inputs), which))

    wk = lookup_projection[0].reshape(2 * N_CHIPS, BLOCK, WIDE)
    wv = content_projection[0].reshape(2 * N_CHIPS, BLOCK, WIDE)
    f_keep, f_sent = pick(which, final_projection[0])
    f_got = swap(f_sent, "core")
    gain = rescaling_factors.reshape(2 * N_CHIPS, 1, BLOCK)
    gate = write_gate_projection[0].T.reshape(HEADS, 2 * N_CHIPS, BLOCK).transpose(1, 0, 2)
    gate = jnp.pad(gate, ((0, 0), (0, GATE_ROWS - HEADS), (0, 0)))

    a = associative_stores[0]
    z = denominator_vectors[0]
    clear = jnp.zeros((FLAG_ROWS, BLOCK), jnp.bfloat16)
    entering = [
        jnp.concatenate(
            [arriving_pieces[t * SEG : (t + 1) * SEG], recall_embeddings, clear], axis=0
        )
        for t in range(steps - 1)
    ]
    for t in range(steps):
        write = t + 1 < steps
        if t > 0:
            moved = next_section(jnp.concatenate([x, tile], axis=0))
            entered = jnp.where(section_zero, entering[t - 1], moved)
            outgoing = copies(entered[:PIECE])
        own = exchange(outgoing)
        got = swap(own, "core")
        begun = project_first(which, own, gain, wk, wv, gate, write, t == 0)
        read, f_near, tile, *state = read_memory(
            which, entered, begun, got, gain, wk, wv, gate, f_got, a, z, write, t == 0
        )
        if write:
            a, z = state
        if t == 0:
            read, entering, section_zero = lax.optimization_barrier((read, entering, section_zero))
        p = exchange(output(read, swap(read, "core"), f_keep, f_near))
        total = jnp.sum(p.astype(jnp.float32), axis=0)
        x = (entered[:PIECE].astype(jnp.float32) + total).astype(jnp.bfloat16)
    return x


def solution(mesh):
    fine = Mesh(mesh.devices.reshape(2, 8, 4, 2, 2), AXES)
    return jax.shard_map(
        local,
        mesh=fine,
        in_specs=(
            P(SECTION, TENSOR),
            P(SECTION),
            P(None, TENSOR),
            P(None, TENSOR),
            P(SECTION, None),
            P(SECTION, None, TENSOR),
            P(SECTION, None, TENSOR),
            P(SECTION, None, TENSOR),
            P(SECTION, TENSOR, None),
            P(SECTION, TENSOR, None, None),
            P(SECTION, TENSOR, None),
        ),
        out_specs=P(SECTION, TENSOR),
        check_vma=False,
    )
```
